32 devices in a mesh: dom: 8 (over y, x, core), shard: 4 (over z).
Axes of the slice: x: 2, y: 2, z: 4, core: 2. Of those that a mesh axis runs over, the one named last changes fastest.
Arguments:
- lhs_emb: bfloat16 [8192, 400], P(('dom', 'shard')), may hold values from -4 to 4
- lhs_acc: float32 [8192], P(('dom', 'shard')), may hold values from 0.05 to 1
- rhs_emb: bfloat16 [8192, 400], P(('dom', 'shard')), may hold values from -4 to 4
- rhs_acc: float32 [8192], P(('dom', 'shard')), may hold values from 0.05 to 1
- operators: float32 [2, 400, 400], replicated, may hold values from -2 to 2
- operator_acc: float32 [2, 400], replicated, may hold values from 65.536 to 1966.08
- partner_mask: int32 [1], replicated, may hold values from 1 to 7
- edge_lhs: int32 [512, 128], P(('dom', 'shard')), may hold values from 0 to 1023
- edge_rhs: int32 [512, 128], P(('dom', 'shard')), may hold values from 0 to 1023
- negatives: int32 [512, 128], P(('dom', 'shard')), may hold values from 0 to 1023
- block_relation: int32 [512], P(('dom', 'shard')), may hold values from 0 to 1
- edge_count: int32 [32], P(('dom', 'shard')), may hold values from 1 to 2048, as said below
Outputs:
- new_lhs: bfloat16 [8192, 400], P(('dom', 'shard'))
- new_lhs_acc: float32 [8192], P(('dom', 'shard'))
- new_rhs: bfloat16 [8192, 400], P(('dom', 'shard'))
- new_rhs_acc: float32 [8192], P(('dom', 'shard'))
- new_operators: float32 [2, 400, 400], replicated
- new_operator_acc: float32 [2, 400], replicated
The draws below stay inside these ranges and needn't reach their ends.
Inputs may be any that keep to these rules, and one draw needn't show every extreme that they name: `edge_count`: the live edges of a device fill the first slots of its blocks, block after block; in every draw some device is full with 2048 live edges.
All inputs are finite; a program needn't handle non-finite values.
Results may differ from the reference program's by a relative error of at most 0.0058.
Values may be sent and summed in bfloat16 or wider, within the bound.
A program may use at most 64 MiB of HBM per device.

```python
import math
import jax
import jax.numpy as jnp
from jax import lax

D = 400
NREL = 2
SPAN = 128
NEG = 128
BLK_DEV = 16
PART = 1024
ROWS = 8192
BLOCKS = 512
N_DOM = 8
N_SHARD = 4


def draw_lhs_emb(key, part):
    key = jax.random.fold_in(key, 11)
    noise_key = jax.random.fold_in(key, 0)
    values = 0.3 * jax.random.normal(noise_key, (ROWS, D), jnp.float32)
    return jnp.clip(values, -4.0, 4.0).astype(jnp.bfloat16)


def draw_rhs_emb(key, part):
    key = jax.random.fold_in(key, 12)
    noise_key = jax.random.fold_in(key, 0)
    values = 0.3 * jax.random.normal(noise_key, (ROWS, D), jnp.float32)
    return jnp.clip(values, -4.0, 4.0).astype(jnp.bfloat16)


def draw_operators(key, part):
    key = jax.random.fold_in(key, 13)
    values = jax.random.normal(key, (NREL, D, D), jnp.float32) * D ** (-0.5)
    return jnp.clip(values, -2.0, 2.0)


def draw_edge_count(key, part):
    key = jax.random.fold_in(key, 7)
    count_key, pick_key = jax.random.split(key)
    capacity = BLK_DEV * SPAN
    device_total = BLOCKS // BLK_DEV
    raw_draw = jax.random.randint(count_key, (device_total,), 1, capacity + 1)
    counts = jnp.maximum(raw_draw * raw_draw // capacity, 1)
    chosen = jax.random.randint(pick_key, (), 0, device_total)
    return jnp.where(jnp.arange(device_total) == chosen, capacity, counts).astype(jnp.int32)


def place_ends(drawn, rng, least, largest):
    index_at = [jax.random.randint(jax.random.fold_in(rng, axis), (), 0, length) for axis, length in enumerate(drawn.shape)]
    longest = drawn.shape.index(max(drawn.shape))
    next_to = index_at[:longest] + [(index_at[longest] + 1) % drawn.shape[longest]] + index_at[longest + 1:]
    return drawn.at[tuple(index_at)].set(least).at[tuple(next_to)].set(largest)


def level_of(own_key, extent, cuts, smallest, top_value):
    factor_of, own = 1.0, jax.random.fold_in(own_key, 6)
    for dim, parts in cuts:
        heights = jnp.exp(jax.random.uniform(jax.random.fold_in(own, dim), (parts,), jnp.float32, smallest / len(cuts), top_value / len(cuts)))
        factor_of = factor_of * jnp.repeat(heights, extent[dim] // parts).reshape([-1 if axis == dim else 1 for axis in range(len(extent))])
    return factor_of


def setup_inputs(seed: int = 0) -> dict:
    streams_of = jax.random.split(jax.random.key(seed), 13)
    return {
        "lhs_emb": draw_lhs_emb(jax.random.fold_in(streams_of[12], 71), 0),
        "lhs_acc": jnp.clip(jnp.exp(math.log(1.0) - 2.9957323 * jax.random.uniform(streams_of[1], (ROWS,), jnp.float32) ** level_of(streams_of[1], (ROWS,), ((0, 32),), -0.2, 0.2)), 0.05, 1.0),
        "rhs_emb": draw_rhs_emb(jax.random.fold_in(streams_of[12], 71), 0),
        "rhs_acc": jnp.clip(jnp.exp(math.log(1.0) - 2.9957323 * jax.random.uniform(streams_of[3], (ROWS,), jnp.float32) ** level_of(streams_of[3], (ROWS,), ((0, 32),), -0.2, 0.2)), 0.05, 1.0),
        "operators": draw_operators(jax.random.fold_in(streams_of[12], 71), 0),
        "operator_acc": jnp.clip(jnp.exp(jax.random.uniform(streams_of[5], (NREL, D), jnp.float32, math.log(65.536), math.log(1966.08))), 65.536, 1966.08),
        "partner_mask": jax.random.randint(streams_of[6], (1,), 1, N_DOM).astype(jnp.int32),
        "edge_lhs": place_ends(jax.random.randint(streams_of[7], (BLOCKS, SPAN), 0, PART), jax.random.fold_in(streams_of[7], 1), 0, PART - 1).astype(jnp.int32),
        "edge_rhs": place_ends(jax.random.randint(streams_of[8], (BLOCKS, SPAN), 0, PART), jax.random.fold_in(streams_of[8], 1), 0, PART - 1).astype(jnp.int32),
        "negatives": place_ends(jax.random.randint(streams_of[9], (BLOCKS, NEG), 0, PART), jax.random.fold_in(streams_of[9], 1), 0, PART - 1).astype(jnp.int32),
        "block_relation": place_ends(jax.random.randint(streams_of[10], (BLOCKS,), 0, NREL), jax.random.fold_in(streams_of[10], 1), 0, NREL - 1).astype(jnp.int32),
        "edge_count": draw_edge_count(jax.random.fold_in(streams_of[12], 71), 0),
    }


LEARN_RATE = 0.1

def block_terms(left_rows, candidates, operator_low, live_count):
    projected = jnp.dot(left_rows, operator_low, preferred_element_type=jnp.float32).astype(jnp.bfloat16)
    scores = lax.dot_general(projected, candidates, (((1,), (1,)), ((), ())), preferred_element_type=jnp.float32)
    positions = jnp.arange(left_rows.shape[0], dtype=jnp.int32)
    columns = jnp.arange(candidates.shape[0], dtype=jnp.int32)
    column_live = (columns < live_count) | (columns >= left_rows.shape[0])
    row_live = positions < live_count
    masked = jnp.where(column_live[None, :], scores, -jnp.inf)
    row_top = lax.optimization_barrier(jnp.max(masked, axis=1, keepdims=True))
    exp_scores = jnp.exp(masked - row_top)
    soft_weights = exp_scores / lax.optimization_barrier(jnp.sum(exp_scores, axis=1, keepdims=True))
    target = (positions[:, None] == columns[None, :]).astype(jnp.float32)
    score_grad = ((soft_weights - target) * row_live[:, None].astype(jnp.float32)).astype(jnp.bfloat16)
    proj_grad = jnp.dot(score_grad, candidates, preferred_element_type=jnp.float32).astype(jnp.bfloat16)
    cand_grad = lax.dot_general(score_grad, projected, (((0,), (0,)), ((), ())), preferred_element_type=jnp.float32)
    left_grad = lax.dot_general(proj_grad, operator_low, (((1,), (1,)), ((), ())), preferred_element_type=jnp.float32)
    oper_grad = lax.dot_general(left_rows, proj_grad, (((0,), (0,)), ((), ())), preferred_element_type=jnp.float32)
    return (left_grad, cand_grad, oper_grad)

def row_adagrad(weights_in, state_in, grad_in):
    new_state = state_in + lax.optimization_barrier(jnp.mean(grad_in * grad_in, axis=-1))
    updated = weights_in.astype(jnp.float32) - LEARN_RATE * grad_in / jnp.sqrt(new_state)[..., None]
    return (updated, new_state)

def reference(lhs_emb, lhs_acc, rhs_emb, rhs_acc, operators, operator_acc, partner_mask, edge_lhs, edge_rhs, negatives, block_relation, edge_count):
    operator_low = operators.astype(jnp.bfloat16)
    partner_bits = partner_mask[0]
    device_count = N_DOM * N_SHARD

    def device_step(device_index, outer_carry):
        partition = device_index // N_SHARD
        partner = jnp.bitwise_xor(partition, partner_bits)
        left_base = partition * PART
        right_base = partner * PART
        live_edges = edge_count[device_index]
        block_total = (live_edges + SPAN - 1) // SPAN

        def block_step(block_index, inner_carry):
            grad_left, grad_right, grad_oper = inner_carry
            flat_index = device_index * BLK_DEV + block_index
            left_index = edge_lhs[flat_index] + left_base
            right_index = jnp.concatenate([edge_rhs[flat_index], negatives[flat_index]]) + right_base
            relation = block_relation[flat_index]
            left_rows = jnp.take(lhs_emb, left_index, axis=0)
            candidates = jnp.take(rhs_emb, right_index, axis=0)
            left_grad, cand_grad, oper_grad = block_terms(left_rows, candidates, operator_low[relation], live_edges - block_index * SPAN)
            grad_left = grad_left.at[left_index].add(left_grad)
            grad_right = grad_right.at[right_index].add(cand_grad)
            grad_oper = grad_oper.at[relation].add(oper_grad)
            return (grad_left, grad_right, grad_oper)
        return lax.fori_loop(jnp.int32(0), block_total, block_step, outer_carry)
    zeros_rows = jnp.zeros((ROWS, D), jnp.float32)
    zeros_oper = jnp.zeros((NREL, D, D), jnp.float32)
    grad_left, grad_right, grad_oper = lax.fori_loop(jnp.int32(0), jnp.int32(device_count), device_step, (zeros_rows, zeros_rows, zeros_oper))
    new_lhs, new_lhs_acc = row_adagrad(lhs_emb, lhs_acc, grad_left)
    new_rhs, new_rhs_acc = row_adagrad(rhs_emb, rhs_acc, grad_right)
    new_operators, new_operator_acc = row_adagrad(operators, operator_acc, grad_oper)
    return (new_lhs.astype(jnp.bfloat16), new_lhs_acc, new_rhs.astype(jnp.bfloat16), new_rhs_acc, new_operators, new_operator_acc)
```

```python
import functools

import jax
import jax.numpy as jnp
from jax import lax
from jax.experimental import pallas as pl
from jax.experimental.pallas import tpu as pltpu
from jax.sharding import PartitionSpec as P

D = 400
WIDE = 512
SPAN = 128
LEARN_RATE = 0.1
BF = jnp.bfloat16
F32 = jnp.float32


def from_partner(array, axis, distance):
    return lax.ppermute(array, axis, [(i, i ^ 1 << distance) for i in range(lax.axis_size(axis))])


def row_adagrad(weights_in, state_in, grad_in):
    new_state = state_in + jnp.mean(grad_in * grad_in, axis=-1)
    updated = weights_in.astype(F32) - LEARN_RATE * grad_in / jnp.sqrt(new_state)[..., None]
    return (updated, new_state)


def level_flag(partner_bits, level_bit):
    return jnp.bitwise_and(jnp.right_shift(partner_bits, level_bit), 1) == 1


def move_rows(block_rows, partner_bits):
    groups = lax.axis_size("dom")
    for level_bit in range(groups.bit_length() - 1):
        swapped = from_partner(block_rows, "dom", level_bit)
        block_rows = jnp.where(level_flag(partner_bits, level_bit), swapped, block_rows)
    return block_rows


def dot(a, b, dims):
    return lax.dot_general(a, b, (dims, ((), ())), preferred_element_type=F32)


def as_column(index_row):
    return jnp.transpose(jnp.broadcast_to(index_row, (128, index_row.shape[1])))


def gather_rows(index_row, table):
    part = table.shape[0]
    column = as_column(index_row)
    lanes = lax.broadcasted_iota(jnp.int32, column.shape, 1)
    shifted = column - lanes
    hot = jnp.concatenate(
        [jnp.where(shifted == c * 128, 1.0, 0.0).astype(BF) for c in range(part // 128)], axis=1
    )
    return dot(hot, table[...], ((1,), (0,))).astype(BF)


def scatter_rows(index_row, grads, total):
    part = total.shape[0]
    step = 256
    rows = lax.broadcasted_iota(jnp.int32, (step, index_row.shape[1]), 0)
    shifted = jnp.broadcast_to(index_row, rows.shape) - rows
    for c in range(part // step):
        hot = jnp.where(shifted == c * step, 1.0, 0.0).astype(BF)
        total[pl.ds(c * step, step), :] += dot(hot, grads, ((1,), (0,)))


def bucket_kernel(
    groups,
    blocks,
    info,
    index,
    left_in,
    right_in,
    oper_in,
    left_out,
    right_out,
    oper_out,
    left,
    right,
    oper,
    left_sum,
    right_sum,
    oper_sum,
):
    me = lax.axis_index("shard")
    for wide, narrow in ((left, left_in), (right, right_in)):
        wide[:, 384:] = jnp.zeros((wide.shape[0], WIDE - 384), BF)
        wide[:, :D] = narrow[...]
    oper[...] = jnp.zeros_like(oper)
    oper[:, :D, :D] = oper_in[...].astype(BF)
    left_sum[...] = jnp.zeros_like(left_sum)
    right_sum[...] = jnp.zeros_like(right_sum)
    oper_sum[...] = jnp.zeros_like(oper_sum)

    counts = [info[g * blocks, 1] for g in range(groups)]
    starts = [jnp.int32(0)]
    for g in range(groups):
        starts.append(starts[-1] + (counts[g] + SPAN - 1) // SPAN)
    in_all = starts[-1]
    mine = (in_all - me + groups - 1) // groups

    def locate(step):
        slot = step * groups + me
        exists = slot < in_all
        slot = jnp.minimum(slot, in_all - 1)
        owner = jnp.int32(0)
        start = jnp.int32(0)
        count = counts[0]
        for g in range(1, groups):
            later = slot >= starts[g]
            owner = jnp.where(later, g, owner)
            start = jnp.where(later, starts[g], start)
            count = jnp.where(later, counts[g], count)
        within = slot - start
        flat = owner * blocks + within
        live = jnp.where(exists, count - within * SPAN, 0)
        return flat, info[flat, 0], live

    def visit(pair, carry):
        left_ids, right_ids, left_grads, right_grads = [], [], [], []
        for half in range(2):
            flat, relation, live = locate(pair * 2 + half)
            row = index[pl.ds(flat, 1), :]
            left_id = row[:, :SPAN]
            right_id = row[:, SPAN : 3 * SPAN]
            low = oper[relation]
            left_rows = gather_rows(left_id, left)
            candidates = gather_rows(right_id, right)
            projected = dot(left_rows, low, ((1,), (0,))).astype(BF)
            scores = dot(projected, candidates, ((1,), (1,)))
            rows = lax.broadcasted_iota(jnp.int32, scores.shape, 0)
            columns = lax.broadcasted_iota(jnp.int32, scores.shape, 1)
            column_live = (columns < live) | (columns >= SPAN)
            masked = jnp.where(column_live, scores, -jnp.inf)
            row_top = jnp.max(masked, axis=1, keepdims=True)
            exp_scores = jnp.exp(masked - row_top)
            soft = exp_scores / jnp.sum(exp_scores, axis=1, keepdims=True)
            grad = soft - jnp.where(rows == columns, 1.0, 0.0)
            score_grad = jnp.where(rows < live, grad, 0.0).astype(BF)
            proj_grad = dot(score_grad, candidates, ((1,), (0,))).astype(BF)
            cand_grad = dot(score_grad, projected, ((0,), (0,)))
            left_grad = dot(proj_grad, low, ((1,), (1,)))
            oper_sum[relation] += dot(left_rows, proj_grad, ((0,), (0,)))
            left_ids.append(left_id)
            right_ids.append(right_id)
            left_grads.append(left_grad.astype(BF))
            right_grads.append(cand_grad.astype(BF))
        join = lambda parts, axis: jnp.concatenate(parts, axis=axis)
        scatter_rows(join(left_ids, 1), join(left_grads, 0), left_sum)
        scatter_rows(join(right_ids, 1), join(right_grads, 0), right_sum)
        return carry

    lax.fori_loop(0, (mine + 1) // 2, visit, 0)
    left_out[...] = left_sum[:, :D].astype(BF)
    right_out[...] = right_sum[:, :D].astype(BF)
    oper_out[...] = oper_sum[:, :D, :D]


def bucket(packed, left_part, right_part, operators):
    groups = lax.axis_size("shard")
    total, _ = packed.shape
    part = left_part.shape[0]
    whole = lambda shape: pl.BlockSpec(shape, lambda i: (0,) * len(shape))
    nrel = operators.shape[0]
    return pl.pallas_call(
        functools.partial(bucket_kernel, groups, total // groups),
        grid=(1,),
        in_specs=[
            pl.BlockSpec((total, 128), lambda i: (0, 3), memory_space=pltpu.SMEM),
            whole(packed.shape),
            whole(left_part.shape),
            whole(right_part.shape),
            whole(operators.shape),
        ],
        out_specs=[whole((part, D)), whole((part, D)), whole(operators.shape)],
        out_shape=[
            jax.ShapeDtypeStruct((part, D), BF),
            jax.ShapeDtypeStruct((part, D), BF),
            jax.ShapeDtypeStruct(operators.shape, F32),
        ],
        scratch_shapes=[
            pltpu.VMEM((part, WIDE), BF),
            pltpu.VMEM((part, WIDE), BF),
            pltpu.VMEM((nrel, WIDE, WIDE), BF),
            pltpu.VMEM((part, WIDE), F32),
            pltpu.VMEM((part, WIDE), F32),
            pltpu.VMEM((nrel, WIDE, WIDE), F32),
        ],
        compiler_params=pltpu.CompilerParams(vmem_limit_bytes=48 * 1024 * 1024),
        name="bucket",
    )(packed, packed, left_part, right_part, operators)


def per_device(
    lhs_emb,
    lhs_acc,
    rhs_emb,
    rhs_acc,
    operators,
    operator_acc,
    partner_mask,
    edge_lhs,
    edge_rhs,
    negatives,
    block_relation,
    edge_count,
):
    partner_bits = partner_mask[0]
    blocks = block_relation.shape[0]
    lane = lax.broadcasted_iota(jnp.int32, (blocks, 128), 1)
    info = jnp.where(lane == 0, block_relation[:, None], edge_count[0])
    packed = jnp.concatenate([edge_lhs, edge_rhs, negatives, info], axis=1)
    packed = lax.all_gather(packed, "shard", axis=0, tiled=True)
    left_part = lax.all_gather(lhs_emb, "shard", axis=0, tiled=True)
    fetched = move_rows(rhs_emb, partner_bits)
    right_part = lax.all_gather(fetched, "shard", axis=0, tiled=True)
    grad_left, grad_right, grad_oper = bucket(packed, left_part, right_part, operators)
    own_left, own_right = (
        lax.psum_scatter(g, "shard", scatter_dimension=0, tiled=True)
        for g in (grad_left, grad_right)
    )
    owner_right = move_rows(own_right, partner_bits)
    new_lhs, new_lhs_acc = row_adagrad(lhs_emb, lhs_acc, own_left.astype(F32))
    new_rhs, new_rhs_acc = row_adagrad(rhs_emb, rhs_acc, owner_right.astype(F32))
    total_oper = lax.psum(grad_oper, ("dom", "shard"))
    new_operators, new_operator_acc = row_adagrad(operators, operator_acc, total_oper)
    return (
        new_lhs.astype(BF),
        new_lhs_acc,
        new_rhs.astype(BF),
        new_rhs_acc,
        new_operators,
        new_operator_acc,
    )


def solution(mesh):
    rows = P(("dom", "shard"), None)
    flat = P(("dom", "shard"))
    in_specs = (rows, flat, rows, flat, P(), P(), P(), rows, rows, rows, flat, flat)
    out_specs = (rows, flat, rows, flat, P(), P())
    return jax.shard_map(
        per_device, mesh=mesh, in_specs=in_specs, out_specs=out_specs, check_vma=False
    )
```

```python
import functools

import jax
import jax.numpy as jnp
from jax import lax
from jax.experimental import pallas as pl
from jax.experimental.pallas import tpu as pltpu
from jax.sharding import PartitionSpec as P

D = 400
WIDE = 512
SPAN = 128
LEARN_RATE = 0.1
BF = jnp.bfloat16
F32 = jnp.float32
MESH = pl.DeviceIdType.MESH


def row_adagrad(weights_in, state_in, grad_in):
    new_state = state_in + jnp.mean(grad_in * grad_in, axis=-1)
    updated = weights_in.astype(F32) - LEARN_RATE * grad_in / jnp.sqrt(new_state)[..., None]
    return (updated, new_state)


def flip(position, bit):
    return position + bit - 2 * bit * ((position // bit) % 2)


def partners(groups):
    dom, shard = lax.axis_index("dom"), lax.axis_index("shard")
    levels = [{"dom": flip(dom, 1 << l)} for l in range(groups.bit_length() - 1)]
    return levels, {"shard": flip(shard, 1)}, {"shard": flip(shard, 2)}


def is_home():
    return lax.axis_index("dom") % 2 == lax.axis_index("shard") // 2


def meet(others):
    barrier = pltpu.get_barrier_semaphore()
    for other in others:
        pl.semaphore_signal(barrier, inc=1, device_id=other, device_id_type=MESH)
    pl.semaphore_wait(barrier, len(others))


def level_orders(levels):
    order = list(range(levels))
    return [order, order[:1] + order[1:][::-1]]


def remote(src, dst, send_sem, recv_sem, other):
    return pltpu.make_async_remote_copy(
        src_ref=src,
        dst_ref=dst,
        send_sem=send_sem,
        recv_sem=recv_sem,
        device_id=other,
        device_id_type=MESH,
    )


class Swaps:
    def __init__(self, levels, mask, held, came, send_sem, recv_sem):
        self.levels, self.mask, self.held, self.came = levels, mask, held, came
        self.send_sem, self.recv_sem = send_sem, recv_sem
        self.orders = level_orders(len(levels))

    def copy(self, half, step):
        return remote(
            self.held.at[half, step],
            self.came.at[half, step],
            self.send_sem.at[half, step],
            self.recv_sem.at[half, step],
            self.levels[self.orders[half][step]],
        )

    def start(self, step):
        for half in range(2):
            self.copy(half, step).start()

    def end(self, step):
        for half in range(2):
            self.copy(half, step).wait()
            bit = 1 << self.orders[half][step]
            flag = (self.mask[0] // bit) % 2
            wide = jnp.full(self.held.shape[2:], flag, jnp.int32)
            self.held[half, step + 1] = jnp.where(
                wide == 1, self.came[half, step].astype(F32), self.held[half, step].astype(F32)
            ).astype(BF)
            if step + 1 < len(self.levels):
                self.copy(half, step + 1).start()

    def put(self, rows):
        half = rows.shape[0] // 2
        for part in range(2):
            self.held[part, 0] = rows[part * half : (part + 1) * half].astype(BF)


def shard_rows(ref, j, rows):
    at = lax.axis_index("shard")
    for bit in (1, 2):
        if j & bit:
            at = flip(at, bit)
    return ref.at[pl.ds(pl.multiple_of(at * rows, rows), rows)]


def collect_kernel(
    groups, mask, lists, left, right, all_lists, all_left, all_right,
    held, came, fetched, dsend, drecv, zsend, csend, recv,
):
    levels, near, far = partners(groups)
    core = levels[0]
    home = is_home()
    away = jnp.logical_not(home)
    sources = (lists, left, fetched)
    totals = (all_lists, all_left, all_right)

    def piece(t, j):
        return shard_rows(totals[t], j, sources[t].shape[0])

    def to_near(t, j):
        return remote(piece(t, j), piece(t, j), zsend.at[t, j], recv.at[t, j + 1], near)

    def to_core(t, j):
        return remote(piece(t, j), piece(t, j), csend.at[t, j], recv.at[t, j], core)

    def to_far(t):
        return remote(sources[t], piece(t, 0), zsend.at[t, 0], recv.at[t, 2], far)

    def begin(t):
        @pl.when(home)
        def _():
            piece(t, 0)[...] = sources[t][...]
            to_near(t, 0).start()
            to_core(t, 0).start()

        @pl.when(away)
        def _():
            to_far(t).start()

    def relay(t):
        @pl.when(home)
        def _():
            to_core(t, 2).wait_recv()
            to_near(t, 2).start()
            to_core(t, 2).start()

    def spread(t):
        @pl.when(home)
        def _():
            for j in (1, 3):
                to_core(t, j).wait_recv()
                to_core(t, j).start()

    def finish(t):
        @pl.when(home)
        def _():
            for j in (0, 2):
                to_near(t, j).wait_send()
            for j in range(4):
                to_core(t, j).wait_send()

        @pl.when(away)
        def _():
            to_far(t).wait_send()
            for j in range(4):
                to_core(t, j).wait_recv()

    swaps = Swaps(levels, mask, held, came, dsend, drecv)
    swaps.put(right)
    meet(levels + [near, far])
    swaps.start(0)
    begin(0)
    begin(1)
    for step in range(len(levels)):
        swaps.end(step)
        if step == 0:
            relay(0)
        if step == min(1, len(levels) - 1):
            relay(1)
    half = fetched.shape[0] // 2
    for part in range(2):
        fetched[part * half : (part + 1) * half, :] = held[part, len(levels)]
    begin(2)
    spread(0)
    spread(1)
    relay(2)
    spread(2)
    for t in range(3):
        finish(t)


def collect(mask, lists, left, right):
    groups, shards = lax.axis_size("dom"), lax.axis_size("shard")
    rows, width = left.shape
    steps = groups.bit_length() - 1
    vmem = pl.BlockSpec(memory_space=pltpu.VMEM)
    dma = pltpu.SemaphoreType.DMA
    return pl.pallas_call(
        functools.partial(collect_kernel, groups),
        in_specs=[pl.BlockSpec(memory_space=pltpu.SMEM)] + [vmem] * 3,
        out_specs=[vmem] * 3,
        out_shape=[
            jax.ShapeDtypeStruct((shards * lists.shape[0], lists.shape[1]), lists.dtype),
            jax.ShapeDtypeStruct((shards * rows, width), BF),
            jax.ShapeDtypeStruct((shards * rows, width), BF),
        ],
        scratch_shapes=[
            pltpu.VMEM((2, steps + 1, rows // 2, width), BF),
            pltpu.VMEM((2, steps, rows // 2, width), BF),
            pltpu.VMEM((rows, width), BF),
            dma((2, steps)),
            dma((2, steps)),
            dma((3, 4)),
            dma((3, 4)),
            dma((3, 4)),
        ],
        compiler_params=pltpu.CompilerParams(
            collective_id=0, has_side_effects=True, vmem_limit_bytes=32 * 1024 * 1024
        ),
        name="collect",
    )(mask, lists, left, right)


def reduce_kernel(
    groups, mask, right, left, oper, own_right, own_left, oper_total,
    held, came, core_in, near_in, far_in, out_going, own_sum, piece_in, work,
    dsend, drecv, csend, crecv, nsend, nrecv, fsend, frecv, osend, orecv, gsend, grecv,
):
    levels, near, far = partners(groups)
    core = levels[0]
    home = is_home()
    away = jnp.logical_not(home)
    totals = (right, left)
    rows = own_right.shape[0]
    dom, shard = lax.axis_index("dom"), lax.axis_index("shard")

    def to_core(t, j):
        return remote(
            shard_rows(totals[t], j, rows), core_in.at[t, j], csend.at[t, j], crecv.at[t, j], core
        )

    def to_near(t, j):
        return remote(
            out_going.at[t, j], near_in.at[t, j // 2], nsend.at[t, j // 2], nrecv.at[t, j // 2], near
        )

    def to_far(t):
        return remote(out_going.at[t, 2], far_in.at[t], fsend.at[t], frecv.at[t], far)

    def begin(t):
        @pl.when(away)
        def _():
            for j in (1, 3, 0, 2):
                to_core(t, j).start()

    def pair_sum(t, j):
        return shard_rows(totals[t], j, rows)[...].astype(F32) + core_in[t, j].astype(F32)

    def first(t):
        @pl.when(home)
        def _():
            for j in (1, 3):
                to_core(t, j).wait_recv()
                out_going[t, j] = pair_sum(t, j).astype(BF)
                to_near(t, j).start()

    def second(t):
        @pl.when(home)
        def _():
            for j in (2, 0):
                to_core(t, j).wait_recv()
                to_near(t, j).wait_recv()
                total = pair_sum(t, j) + near_in[t, j // 2].astype(F32)
                if j == 2:
                    out_going[t, 2] = total.astype(BF)
                    to_far(t).start()
                else:
                    own_sum[t] = total

    def third(t):
        @pl.when(away)
        def _():
            to_far(t).wait_recv()
            own_sum[t] = far_in[t].astype(F32)

    def finish(t):
        @pl.when(home)
        def _():
            for j in (1, 3):
                to_near(t, j).wait_send()
            to_far(t).wait_send()

        @pl.when(away)
        def _():
            for j in range(4):
                to_core(t, j).wait_send()

    every = levels + [near, far]
    bits = [(dom // (1 << l)) % 2 for l in range(len(levels))] + [shard % 2, (shard // 2) % 2]
    spans, starts = [oper.shape[0]], [jnp.int32(0) + shard * 0]
    for l in range(len(every)):
        if spans[-1] >= 32:
            spans.append(spans[-1] // 2)
            starts.append(starts[-1] + bits[l] * spans[-1])
        else:
            spans.append(spans[-1])
            starts.append(starts[-1])
    lands = [0]
    for l in range(len(every)):
        lands.append(lands[-1] + spans[l + 1])

    def window(ref, start, span):
        return ref.at[pl.ds(pl.multiple_of(start, 16), span)]

    def oper_copy(l):
        span = spans[l + 1]
        start = starts[l] + (1 - bits[l]) * span if span < spans[l] else starts[l]
        return remote(
            window(work, start, span), piece_in.at[pl.ds(lands[l], span)], osend.at[l], orecv.at[l], every[l]
        )

    def oper_end(l):
        oper_copy(l).wait()
        span = spans[l + 1]
        at = pl.ds(pl.multiple_of(starts[l + 1], 16), span)
        total = work[at, :].astype(F32) + piece_in[pl.ds(lands[l], span), :].astype(F32)
        work[at, :] = total.astype(BF)

    halved = [l for l in range(len(every)) if spans[l + 1] < spans[l]]

    def back_copy(l):
        part = window(oper_total, starts[l + 1], spans[l + 1])
        return remote(part, part, gsend.at[l], grecv.at[l], every[l])

    swaps = Swaps(levels, mask, held, came, dsend, drecv)
    work[...] = oper[...].astype(BF)
    meet(every)
    begin(0)
    oper_copy(0).start()
    begin(1)
    last = len(every)
    todo = {
        0: lambda: (first(0), first(1)),
        1: lambda: second(0),
        2: lambda: (third(0), swaps.put(own_sum.at[0]), swaps.start(0), second(1)),
    }
    for l in range(last):
        if l in todo:
            todo[l]()
        if l >= 3 and l - 3 < len(levels):
            swaps.end(l - 3)
        oper_end(l)
        if l + 1 < last:
            oper_copy(l + 1).start()
    window(oper_total, starts[-1], spans[-1])[...] = window(work, starts[-1], spans[-1])[...]
    backs = halved[::-1]
    step = last - 3
    for l in backs:
        back_copy(l).start()
        if step < len(levels):
            swaps.end(step)
            step += 1
        back_copy(l).wait()
    for rest in range(step, len(levels)):
        swaps.end(rest)
    half = rows // 2
    for part in range(2):
        own_right[part * half : (part + 1) * half, :] = held[part, len(levels)]
    third(1)
    own_left[...] = own_sum[1]
    for t in range(2):
        finish(t)


def reduce(mask, grad_right, grad_left, grad_oper):
    groups, shards = lax.axis_size("dom"), lax.axis_size("shard")
    part, width = grad_left.shape
    rows = part // shards
    steps = groups.bit_length() - 1
    every = steps + 2
    vmem = pl.BlockSpec(memory_space=pltpu.VMEM)
    dma = pltpu.SemaphoreType.DMA
    return pl.pallas_call(
        functools.partial(reduce_kernel, groups),
        in_specs=[pl.BlockSpec(memory_space=pltpu.SMEM)] + [vmem] * 3,
        out_specs=[vmem] * 3,
        out_shape=[
            jax.ShapeDtypeStruct((rows, width), BF),
            jax.ShapeDtypeStruct((rows, width), F32),
            jax.ShapeDtypeStruct(grad_oper.shape, BF),
        ],
        scratch_shapes=[
            pltpu.VMEM((2, steps + 1, rows // 2, width), BF),
            pltpu.VMEM((2, steps, rows // 2, width), BF),
            pltpu.VMEM((2, 4, rows, width), BF),
            pltpu.VMEM((2, 2, rows, width), BF),
            pltpu.VMEM((2, rows, width), BF),
            pltpu.VMEM((2, 4, rows, width), BF),
            pltpu.VMEM((2, rows, width), F32),
            pltpu.VMEM((grad_oper.shape[0] + 16 * every, width), BF),
            pltpu.VMEM(grad_oper.shape, BF),
            dma((2, steps)),
            dma((2, steps)),
            dma((2, 4)),
            dma((2, 4)),
            dma((2, 2)),
            dma((2, 2)),
            dma((2,)),
            dma((2,)),
            dma((every,)),
            dma((every,)),
            dma((every,)),
            dma((every,)),
        ],
        compiler_params=pltpu.CompilerParams(
            collective_id=1, has_side_effects=True, vmem_limit_bytes=40 * 1024 * 1024
        ),
        name="reduce",
    )(mask, grad_right, grad_left, grad_oper)


def dot(a, b, dims):
    return lax.dot_general(a, b, (dims, ((), ())), preferred_element_type=F32)


def as_column(index_row):
    return jnp.transpose(jnp.broadcast_to(index_row, (128, index_row.shape[1])))


def gather_rows(index_row, table):
    part = table.shape[0]
    column = as_column(index_row)
    lanes = lax.broadcasted_iota(jnp.int32, column.shape, 1)
    shifted = column - lanes
    hot = jnp.concatenate(
        [jnp.where(shifted == c * 128, 1.0, 0.0).astype(BF) for c in range(part // 128)], axis=1
    )
    return dot(hot, table[...], ((1,), (0,))).astype(BF)


def scatter_rows(index_row, grads, total):
    part = total.shape[0]
    step = 256
    rows = lax.broadcasted_iota(jnp.int32, (step, index_row.shape[1]), 0)
    shifted = jnp.broadcast_to(index_row, rows.shape) - rows
    for c in range(part // step):
        hot = jnp.where(shifted == c * step, 1.0, 0.0).astype(BF)
        total[pl.ds(c * step, step), :] += dot(hot, grads, ((1,), (0,)))


def bucket_kernel(
    groups,
    blocks,
    info,
    index,
    left_in,
    right_in,
    oper_in,
    left_out,
    right_out,
    oper_out,
    left,
    right,
    oper,
    left_sum,
    right_sum,
    oper_sum,
):
    me = (lax.axis_index("shard") % 2) * 2 + lax.axis_index("dom") % 2
    for wide, narrow in ((left, left_in), (right, right_in)):
        wide[:, 384:] = jnp.zeros((wide.shape[0], WIDE - 384), BF)
        wide[:, :D] = narrow[...]
    oper[...] = jnp.zeros_like(oper)
    oper[:, :D, :D] = oper_in[...].astype(BF)
    left_sum[...] = jnp.zeros_like(left_sum)
    right_sum[...] = jnp.zeros_like(right_sum)
    oper_sum[...] = jnp.zeros_like(oper_sum)

    counts = [info[g * blocks, 1] for g in range(groups)]
    starts = [jnp.int32(0)]
    for g in range(groups):
        starts.append(starts[-1] + (counts[g] + SPAN - 1) // SPAN)
    in_all = starts[-1]
    mine = (in_all - me + groups - 1) // groups

    def locate(step):
        slot = step * groups + me
        exists = slot < in_all
        slot = jnp.minimum(slot, in_all - 1)
        owner = jnp.int32(0)
        start = jnp.int32(0)
        count = counts[0]
        for g in range(1, groups):
            later = slot >= starts[g]
            owner = jnp.where(later, g, owner)
            start = jnp.where(later, starts[g], start)
            count = jnp.where(later, counts[g], count)
        within = slot - start
        flat = owner * blocks + within
        live = jnp.where(exists, count - within * SPAN, 0)
        return flat, info[flat, 0], live

    def visit(pair, carry):
        left_ids, right_ids, left_grads, right_grads = [], [], [], []
        for half in range(2):
            flat, relation, live = locate(pair * 2 + half)
            row = index[pl.ds(flat, 1), :]
            left_id = row[:, :SPAN]
            right_id = row[:, SPAN : 3 * SPAN]
            low = oper[relation]
            left_rows = gather_rows(left_id, left)
            candidates = gather_rows(right_id, right)
            projected = dot(left_rows, low, ((1,), (0,))).astype(BF)
            scores = dot(projected, candidates, ((1,), (1,)))
            rows = lax.broadcasted_iota(jnp.int32, scores.shape, 0)
            columns = lax.broadcasted_iota(jnp.int32, scores.shape, 1)
            column_live = (columns < live) | (columns >= SPAN)
            masked = jnp.where(column_live, scores, -jnp.inf)
            row_top = jnp.max(masked, axis=1, keepdims=True)
            exp_scores = jnp.exp(masked - row_top)
            soft = exp_scores / jnp.sum(exp_scores, axis=1, keepdims=True)
            grad = soft - jnp.where(rows == columns, 1.0, 0.0)
            score_grad = jnp.where(rows < live, grad, 0.0).astype(BF)
            proj_grad = dot(score_grad, candidates, ((1,), (0,))).astype(BF)
            cand_grad = dot(score_grad, projected, ((0,), (0,)))
            left_grad = dot(proj_grad, low, ((1,), (1,)))
            oper_sum[relation] += dot(left_rows, proj_grad, ((0,), (0,)))
            left_ids.append(left_id)
            right_ids.append(right_id)
            left_grads.append(left_grad.astype(BF))
            right_grads.append(cand_grad.astype(BF))
        join = lambda parts, axis: jnp.concatenate(parts, axis=axis)
        scatter_rows(join(left_ids, 1), join(left_grads, 0), left_sum)
        scatter_rows(join(right_ids, 1), join(right_grads, 0), right_sum)
        return carry

    lax.fori_loop(0, (mine + 1) // 2, visit, 0)
    left_out[...] = left_sum[:, :D].astype(BF)
    right_out[...] = right_sum[:, :D].astype(BF)
    for relation in range(oper_sum.shape[0]):
        oper_out[relation * WIDE : (relation + 1) * WIDE, :] = oper_sum[relation, :, :D]


def bucket(packed, left_part, right_part, operators):
    groups = lax.axis_size("shard")
    total, _ = packed.shape
    part = left_part.shape[0]
    whole = lambda shape: pl.BlockSpec(shape, lambda i: (0,) * len(shape))
    nrel = operators.shape[0]
    return pl.pallas_call(
        functools.partial(bucket_kernel, groups, total // groups),
        grid=(1,),
        in_specs=[
            pl.BlockSpec((total, 128), lambda i: (0, 3), memory_space=pltpu.SMEM),
            whole(packed.shape),
            whole(left_part.shape),
            whole(right_part.shape),
            whole(operators.shape),
        ],
        out_specs=[whole((part, D)), whole((part, D)), whole((nrel * WIDE, D))],
        out_shape=[
            jax.ShapeDtypeStruct((part, D), BF),
            jax.ShapeDtypeStruct((part, D), BF),
            jax.ShapeDtypeStruct((nrel * WIDE, D), F32),
        ],
        scratch_shapes=[
            pltpu.VMEM((part, WIDE), BF),
            pltpu.VMEM((part, WIDE), BF),
            pltpu.VMEM((nrel, WIDE, WIDE), BF),
            pltpu.VMEM((part, WIDE), F32),
            pltpu.VMEM((part, WIDE), F32),
            pltpu.VMEM((nrel, WIDE, WIDE), F32),
        ],
        compiler_params=pltpu.CompilerParams(vmem_limit_bytes=48 * 1024 * 1024),
        name="bucket",
    )(packed, packed, left_part, right_part, operators)


def per_device(
    lhs_emb,
    lhs_acc,
    rhs_emb,
    rhs_acc,
    operators,
    operator_acc,
    partner_mask,
    edge_lhs,
    edge_rhs,
    negatives,
    block_relation,
    edge_count,
):
    blocks = block_relation.shape[0]
    lane = lax.broadcasted_iota(jnp.int32, (blocks, 128), 1)
    info = jnp.where(lane == 0, block_relation[:, None], edge_count[0])
    packed = jnp.concatenate([edge_lhs, edge_rhs, negatives, info], axis=1)
    lists, left_part, right_part = collect(partner_mask, packed, lhs_emb, rhs_emb)
    grad_left, grad_right, grad_oper = bucket(lists, left_part, right_part, operators)
    own_right, own_left, total_oper = reduce(partner_mask, grad_right, grad_left, grad_oper)
    new_lhs, new_lhs_acc = row_adagrad(lhs_emb, lhs_acc, own_left)
    new_rhs, new_rhs_acc = row_adagrad(rhs_emb, rhs_acc, own_right.astype(F32))
    total_oper = total_oper.reshape(operators.shape[0], WIDE, D)[:, :D].astype(F32)
    new_operators, new_operator_acc = row_adagrad(operators, operator_acc, total_oper)
    return (
        new_lhs.astype(BF),
        new_lhs_acc,
        new_rhs.astype(BF),
        new_rhs_acc,
        new_operators,
        new_operator_acc,
    )


def solution(mesh):
    rows = P(("dom", "shard"), None)
    flat = P(("dom", "shard"))
    in_specs = (rows, flat, rows, flat, P(), P(), P(), rows, rows, rows, flat, flat)
    out_specs = (rows, flat, rows, flat, P(), P())
    return jax.shard_map(
        per_device, mesh=mesh, in_specs=in_specs, out_specs=out_specs, check_vma=False
    )
```

```python
import functools

import jax
import jax.numpy as jnp
from jax import lax
from jax.experimental import pallas as pl
from jax.experimental.pallas import tpu as pltpu
from jax.sharding import PartitionSpec as P

D = 400
WIDE = 512
MAIN = 384
REST = D - MAIN
SPAN = 128
LEARN_RATE = 0.1
BF = jnp.bfloat16
F32 = jnp.float32
MESH = pl.DeviceIdType.MESH


def flip(position, bit):
    return position + bit - 2 * bit * ((position // bit) % 2)


def partners(groups):
    dom, shard = lax.axis_index("dom"), lax.axis_index("shard")
    levels = [{"dom": flip(dom, 1 << l)} for l in range(groups.bit_length() - 1)]
    return levels, {"shard": flip(shard, 1)}, {"shard": flip(shard, 2)}


def is_home():
    return lax.axis_index("dom") % 2 == lax.axis_index("shard") // 2


def meet(others):
    barrier = pltpu.get_barrier_semaphore()
    for other in others:
        pl.semaphore_signal(barrier, inc=1, device_id=other, device_id_type=MESH)
    pl.semaphore_wait(barrier, len(others))


def level_orders(levels):
    order = list(range(levels))
    return [order, order[:1] + order[1:][::-1]]


def remote(src, dst, send_sem, recv_sem, other):
    return pltpu.make_async_remote_copy(
        src_ref=src,
        dst_ref=dst,
        send_sem=send_sem,
        recv_sem=recv_sem,
        device_id=other,
        device_id_type=MESH,
    )


def packed_rows(rows):
    return rows + REST


def pack(main, rest):
    turned = jnp.transpose(rest)[:REST, :].astype(BF)
    blank = jnp.zeros((REST, MAIN - turned.shape[1]), BF)
    return main.astype(BF), jnp.concatenate([turned, blank], axis=1)


class Swaps:
    def __init__(self, levels, mask, held, came, send_sem, recv_sem):
        self.levels, self.mask, self.held, self.came = levels, mask, held, came
        self.send_sem, self.recv_sem = send_sem, recv_sem
        self.orders = level_orders(len(levels))

    def copy(self, half, step):
        return remote(
            self.held.at[half, step],
            self.came.at[half, step],
            self.send_sem.at[half, step],
            self.recv_sem.at[half, step],
            self.levels[self.orders[half][step]],
        )

    def start(self, step):
        for half in range(2):
            self.copy(half, step).start()

    def end(self, step):
        for half in range(2):
            self.copy(half, step).wait()
            bit = 1 << self.orders[half][step]
            flag = (self.mask[0] // bit) % 2
            wide = jnp.full(self.held.shape[2:], flag, jnp.int32)
            self.held[half, step + 1] = jnp.where(
                wide == 1, self.came[half, step].astype(F32), self.held[half, step].astype(F32)
            ).astype(BF)
            if step + 1 < len(self.levels):
                self.copy(half, step + 1).start()

    def put(self, rows):
        half = rows.shape[0] // 2
        for part in range(2):
            self.held[part, 0] = rows[part * half : (part + 1) * half].astype(BF)


def shard_rows(ref, j, rows):
    at = lax.axis_index("shard")
    for bit in (1, 2):
        if j & bit:
            at = flip(at, bit)
    return ref.at[pl.ds(pl.multiple_of(at * rows, rows), rows)]


def collect_kernel(
    groups, mask, lists, left, right, all_lists, all_left, all_right,
    held, came, fetched, mine, rest, dsend, drecv, zsend, csend, recv,
):
    levels, near, far = partners(groups)
    core = levels[0]
    home = is_home()
    away = jnp.logical_not(home)
    sources = (lists, mine, fetched)
    rows = left.shape[0]
    totals = (all_lists, all_left, all_right)

    def piece(t, j):
        return shard_rows(totals[t], j, sources[t].shape[0])

    def to_near(t, j):
        return remote(piece(t, j), piece(t, j), zsend.at[t, j], recv.at[t, j + 1], near)

    def to_core(t, j):
        return remote(piece(t, j), piece(t, j), csend.at[t, j], recv.at[t, j], core)

    def to_far(t):
        return remote(sources[t], piece(t, 0), zsend.at[t, 0], recv.at[t, 2], far)

    def begin(t):
        @pl.when(home)
        def _():
            piece(t, 0)[...] = sources[t][...]
            to_near(t, 0).start()
            to_core(t, 0).start()

        @pl.when(away)
        def _():
            to_far(t).start()

    def relay(t):
        @pl.when(home)
        def _():
            to_core(t, 2).wait_recv()
            to_near(t, 2).start()
            to_core(t, 2).start()

    def spread(t):
        @pl.when(home)
        def _():
            for j in (1, 3):
                to_core(t, j).wait_recv()
                to_core(t, j).start()

    def finish(t):
        @pl.when(home)
        def _():
            for j in (0, 2):
                to_near(t, j).wait_send()
            for j in range(4):
                to_core(t, j).wait_send()

        @pl.when(away)
        def _():
            to_far(t).wait_send()
            for j in range(4):
                to_core(t, j).wait_recv()

    swaps = Swaps(levels, mask, held, came, dsend, drecv)
    for raw, whole in ((right, fetched), (left, mine)):
        rest[...] = jnp.zeros_like(rest)
        rest[:, :REST] = raw[:, MAIN:].astype(F32)
        whole[:rows, :], whole[rows:, :] = pack(raw[:, :MAIN], rest[...])
    swaps.put(fetched)
    meet(levels + [near, far])
    swaps.start(0)
    begin(0)
    begin(1)
    for step in range(len(levels)):
        swaps.end(step)
        if step == 0:
            relay(0)
        if step == min(1, len(levels) - 1):
            relay(1)
    half = fetched.shape[0] // 2
    for part in range(2):
        fetched[part * half : (part + 1) * half, :] = held[part, len(levels)]
    begin(2)
    spread(0)
    spread(1)
    relay(2)
    spread(2)
    for t in range(3):
        finish(t)


def collect(mask, lists, left, right):
    groups, shards = lax.axis_size("dom"), lax.axis_size("shard")
    rows, width = packed_rows(left.shape[0]), MAIN
    steps = groups.bit_length() - 1
    vmem = pl.BlockSpec(memory_space=pltpu.VMEM)
    dma = pltpu.SemaphoreType.DMA
    return pl.pallas_call(
        functools.partial(collect_kernel, groups),
        in_specs=[pl.BlockSpec(memory_space=pltpu.SMEM)] + [vmem] * 3,
        out_specs=[vmem] * 3,
        out_shape=[
            jax.ShapeDtypeStruct((shards * lists.shape[0], lists.shape[1]), lists.dtype),
            jax.ShapeDtypeStruct((shards * rows, width), BF),
            jax.ShapeDtypeStruct((shards * rows, width), BF),
        ],
        scratch_shapes=[
            pltpu.VMEM((2, steps + 1, rows // 2, width), BF),
            pltpu.VMEM((2, steps, rows // 2, width), BF),
            pltpu.VMEM((rows, width), BF),
            pltpu.VMEM((rows, width), BF),
            pltpu.VMEM((left.shape[0], 128), F32),
            dma((2, steps)),
            dma((2, steps)),
            dma((3, 4)),
            dma((3, 4)),
            dma((3, 4)),
        ],
        compiler_params=pltpu.CompilerParams(
            collective_id=0, has_side_effects=True, vmem_limit_bytes=32 * 1024 * 1024
        ),
        name="collect",
    )(mask, lists, left, right)


def reduce_kernel(
    groups, mask, right, left, oper, own_right, own_left, oper_total,
    held, came, core_in, near_in, far_in, out_going, own_sum, piece_in, leaving, work,
    dsend, drecv, csend, crecv, nsend, nrecv, fsend, frecv, osend, orecv, gsend, grecv,
):
    levels, near, far = partners(groups)
    core = levels[0]
    home = is_home()
    away = jnp.logical_not(home)
    totals = (right, left)
    rows = own_right.shape[0]
    dom, shard = lax.axis_index("dom"), lax.axis_index("shard")

    def to_core(t, j):
        return remote(
            shard_rows(totals[t], j, rows), core_in.at[t, j], csend.at[t, j], crecv.at[t, j], core
        )

    def to_near(t, j):
        return remote(
            out_going.at[t, j], near_in.at[t, j // 2], nsend.at[t, j // 2], nrecv.at[t, j // 2], near
        )

    def to_far(t):
        return remote(out_going.at[t, 2], far_in.at[t], fsend.at[t], frecv.at[t], far)

    def begin(t):
        @pl.when(away)
        def _():
            for j in (1, 3, 0, 2):
                to_core(t, j).start()

    def pair_sum(t, j):
        return shard_rows(totals[t], j, rows)[...].astype(F32) + core_in[t, j].astype(F32)

    def first(t):
        @pl.when(home)
        def _():
            for j in (1, 3):
                to_core(t, j).wait_recv()
                out_going[t, j] = pair_sum(t, j).astype(BF)
                to_near(t, j).start()

    def second(t):
        @pl.when(home)
        def _():
            for j in (2, 0):
                to_core(t, j).wait_recv()
                to_near(t, j).wait_recv()
                total = pair_sum(t, j) + near_in[t, j // 2].astype(F32)
                if j == 2:
                    out_going[t, 2] = total.astype(BF)
                    to_far(t).start()
                else:
                    own_sum[t] = total

    def third(t):
        @pl.when(away)
        def _():
            to_far(t).wait_recv()
            own_sum[t] = far_in[t].astype(F32)

    def finish(t):
        @pl.when(home)
        def _():
            for j in (1, 3):
                to_near(t, j).wait_send()
            to_far(t).wait_send()

        @pl.when(away)
        def _():
            for j in range(4):
                to_core(t, j).wait_send()

    every = levels + [near, far]
    bits = [(dom // (1 << l)) % 2 for l in range(len(levels))] + [shard % 2, (shard // 2) % 2]
    last = len(every)
    tail = list(range(len(levels), last))
    chains = [order + tail for order in level_orders(len(levels))]
    nrel = work.shape[0]
    spans, lands = [work.shape[1]], [0]
    for step in range(last):
        spans.append(spans[-1] // 2 if spans[-1] >= 32 else spans[-1])
        lands.append(lands[-1] + spans[-1])
    starts = []
    for r in range(nrel):
        at = [shard * 0]
        for step in range(last):
            halves = spans[step + 1] < spans[step]
            at.append(at[-1] + bits[chains[r % 2][step]] * spans[step + 1] if halves else at[-1])
        starts.append(at)

    def window(ref, r, start, span):
        return ref.at[r, pl.ds(pl.multiple_of(start, 16), span)]

    def oper_copy(r, step):
        land = pl.ds(lands[step], spans[step + 1])
        return remote(
            leaving.at[r, land],
            piece_in.at[r, land],
            osend.at[r, step],
            orecv.at[r, step],
            every[chains[r % 2][step]],
        )

    def oper_start(step):
        for r in range(nrel):
            span, start = spans[step + 1], starts[r][step]
            if span < spans[step]:
                start = start + (1 - bits[chains[r % 2][step]]) * span
            leaving[r, pl.ds(lands[step], span)] = window(work, r, start, span)[...].astype(BF)
            oper_copy(r, step).start()

    def oper_end(step):
        for r in range(nrel):
            oper_copy(r, step).wait()
            span = spans[step + 1]
            land = pl.ds(lands[step], span)
            own = window(work, r, starts[r][step + 1], span)
            kept = own[...] if span < spans[step] else leaving[r, land].astype(F32)
            own[...] = kept + piece_in[r, land].astype(F32)

    def back_copy(r, step):
        part = window(oper_total, r, starts[r][step + 1], spans[step + 1])
        return remote(part, part, gsend.at[r, step], grecv.at[r, step], every[chains[r % 2][step]])

    swaps = Swaps(levels, mask, held, came, dsend, drecv)
    work[...] = oper[...]
    meet(every)
    begin(0)
    oper_start(0)
    begin(1)
    todo = {
        0: lambda: (first(0), first(1)),
        1: lambda: second(0),
        2: lambda: (third(0), swaps.put(own_sum.at[0]), swaps.start(0), second(1)),
    }
    for step in range(last):
        if step in todo:
            todo[step]()
        if 3 <= step < 3 + len(levels):
            swaps.end(step - 3)
        oper_end(step)
        if step + 1 < last:
            oper_start(step + 1)
    for r in range(nrel):
        final = window(work, r, starts[r][-1], spans[-1])[...]
        window(oper_total, r, starts[r][-1], spans[-1])[...] = final.astype(BF)
    swap = last - 3
    for step in reversed(range(last)):
        if spans[step + 1] == spans[step]:
            continue
        for r in range(nrel):
            back_copy(r, step).start()
        if swap < len(levels):
            swaps.end(swap)
            swap += 1
        for r in range(nrel):
            back_copy(r, step).wait()
    for rest in range(swap, len(levels)):
        swaps.end(rest)
    half = rows // 2
    for part in range(2):
        own_right[part * half : (part + 1) * half, :] = held[part, len(levels)]
    third(1)
    own_left[...] = own_sum[1]
    for t in range(2):
        finish(t)


def reduce(mask, grad_right, grad_left, grad_oper):
    groups, shards = lax.axis_size("dom"), lax.axis_size("shard")
    part, width = grad_left.shape
    rows = part // shards
    steps = groups.bit_length() - 1
    every = steps + 2
    nrel = grad_oper.shape[0]
    vmem = pl.BlockSpec(memory_space=pltpu.VMEM)
    dma = pltpu.SemaphoreType.DMA
    return pl.pallas_call(
        functools.partial(reduce_kernel, groups),
        in_specs=[pl.BlockSpec(memory_space=pltpu.SMEM)] + [vmem] * 3,
        out_specs=[vmem] * 3,
        out_shape=[
            jax.ShapeDtypeStruct((rows, width), BF),
            jax.ShapeDtypeStruct((rows, width), F32),
            jax.ShapeDtypeStruct(grad_oper.shape, BF),
        ],
        scratch_shapes=[
            pltpu.VMEM((2, steps + 1, rows // 2, width), BF),
            pltpu.VMEM((2, steps, rows // 2, width), BF),
            pltpu.VMEM((2, 4, rows, width), BF),
            pltpu.VMEM((2, 2, rows, width), BF),
            pltpu.VMEM((2, rows, width), BF),
            pltpu.VMEM((2, 4, rows, width), BF),
            pltpu.VMEM((2, rows, width), F32),
            pltpu.VMEM((nrel, grad_oper.shape[1] + 16 * every, width), BF),
            pltpu.VMEM((nrel, grad_oper.shape[1] + 16 * every, width), BF),
            pltpu.VMEM(grad_oper.shape, F32),
            dma((2, steps)),
            dma((2, steps)),
            dma((2, 4)),
            dma((2, 4)),
            dma((2, 2)),
            dma((2, 2)),
            dma((2,)),
            dma((2,)),
            dma((nrel, every)),
            dma((nrel, every)),
            dma((nrel, every)),
            dma((nrel, every)),
        ],
        compiler_params=pltpu.CompilerParams(
            collective_id=1, has_side_effects=True, vmem_limit_bytes=40 * 1024 * 1024
        ),
        name="reduce",
    )(mask, grad_right, grad_left, grad_oper)


def dot(a, b, dims):
    return lax.dot_general(a, b, (dims, ((), ())), preferred_element_type=F32)


def as_column(index_row):
    return jnp.transpose(jnp.broadcast_to(index_row, (128, index_row.shape[1])))


def gather_rows(index_row, table):
    part = table.shape[0]
    column = as_column(index_row)
    lanes = lax.broadcasted_iota(jnp.int32, column.shape, 1)
    shifted = column - lanes
    hot = jnp.concatenate(
        [jnp.where(shifted == c * 128, 1.0, 0.0).astype(BF) for c in range(part // 128)], axis=1
    )
    return dot(hot, table[...], ((1,), (0,))).astype(BF)


def scatter_rows(index_row, grads, total):
    part = total.shape[0]
    step = 256
    rows = lax.broadcasted_iota(jnp.int32, (step, index_row.shape[1]), 0)
    shifted = jnp.broadcast_to(index_row, rows.shape) - rows
    for c in range(part // step):
        hot = jnp.where(shifted == c * step, 1.0, 0.0).astype(BF)
        total[pl.ds(c * step, step), :] += dot(hot, grads, ((1,), (0,)))


def bucket_kernel(
    groups,
    blocks,
    info,
    index,
    left_in,
    right_in,
    oper_in,
    left_out,
    right_out,
    oper_out,
    left,
    right,
    oper,
    left_sum,
    right_sum,
    oper_sum,
    turn,
):
    me = (lax.axis_index("shard") % 2) * 2 + lax.axis_index("dom") % 2
    rows = left.shape[0] // groups
    packs = packed_rows(rows)
    for wide, packed in ((left, left_in), (right, right_in)):
        turn[...] = jnp.zeros_like(turn)
        for g in range(groups):
            wide[g * rows : (g + 1) * rows, :MAIN] = packed[g * packs : g * packs + rows, :]
            turn[:REST, :rows] = packed[g * packs + rows : (g + 1) * packs, :rows].astype(F32)
            wide[g * rows : (g + 1) * rows, MAIN:] = jnp.transpose(turn[:, :rows]).astype(BF)
    oper[...] = jnp.zeros_like(oper)
    oper[:, :D, :D] = oper_in[...].astype(BF)
    left_sum[...] = jnp.zeros_like(left_sum)
    right_sum[...] = jnp.zeros_like(right_sum)
    oper_sum[...] = jnp.zeros_like(oper_sum)

    counts = [info[g * blocks, 1] for g in range(groups)]
    starts = [jnp.int32(0)]
    for g in range(groups):
        starts.append(starts[-1] + (counts[g] + SPAN - 1) // SPAN)
    in_all = starts[-1]
    mine = (in_all - me + groups - 1) // groups

    def locate(step):
        slot = step * groups + me
        exists = slot < in_all
        slot = jnp.minimum(slot, in_all - 1)
        owner = jnp.int32(0)
        start = jnp.int32(0)
        count = counts[0]
        for g in range(1, groups):
            later = slot >= starts[g]
            owner = jnp.where(later, g, owner)
            start = jnp.where(later, starts[g], start)
            count = jnp.where(later, counts[g], count)
        within = slot - start
        flat = owner * blocks + within
        live = jnp.where(exists, count - within * SPAN, 0)
        return flat, info[flat, 0], live

    def visit(pair, carry):
        left_ids, right_ids, left_grads, right_grads = [], [], [], []
        for half in range(2):
            flat, relation, live = locate(pair * 2 + half)
            row = index[pl.ds(flat, 1), :]
            left_id = row[:, :SPAN]
            right_id = row[:, SPAN : 3 * SPAN]
            low = oper[relation]
            left_rows = gather_rows(left_id, left)
            candidates = gather_rows(right_id, right)
            projected = dot(left_rows, low, ((1,), (0,))).astype(BF)
            scores = dot(projected, candidates, ((1,), (1,)))
            rows = lax.broadcasted_iota(jnp.int32, scores.shape, 0)
            columns = lax.broadcasted_iota(jnp.int32, scores.shape, 1)
            column_live = (columns < live) | (columns >= SPAN)
            masked = jnp.where(column_live, scores, -jnp.inf)
            row_top = jnp.max(masked, axis=1, keepdims=True)
            exp_scores = jnp.exp(masked - row_top)
            soft = exp_scores / jnp.sum(exp_scores, axis=1, keepdims=True)
            grad = soft - jnp.where(rows == columns, 1.0, 0.0)
            score_grad = jnp.where(rows < live, grad, 0.0).astype(BF)
            proj_grad = dot(score_grad, candidates, ((1,), (0,))).astype(BF)
            cand_grad = dot(score_grad, projected, ((0,), (0,)))
            left_grad = dot(proj_grad, low, ((1,), (1,)))
            oper_sum[relation] += dot(left_rows, proj_grad, ((0,), (0,)))
            left_ids.append(left_id)
            right_ids.append(right_id)
            left_grads.append(left_grad.astype(BF))
            right_grads.append(cand_grad.astype(BF))
        join = lambda parts, axis: jnp.concatenate(parts, axis=axis)
        scatter_rows(join(left_ids, 1), join(left_grads, 0), left_sum)
        scatter_rows(join(right_ids, 1), join(right_grads, 0), right_sum)
        return carry

    lax.fori_loop(0, (mine + 1) // 2, visit, 0)
    for total, out in ((left_sum, left_out), (right_sum, right_out)):
        for g in range(groups):
            part = total.at[g * rows : (g + 1) * rows]
            at = g * packs
            out[at : at + rows, :], out[at + rows : at + packs, :] = pack(part[:, :MAIN], part[:, MAIN:])
    for relation in range(oper_sum.shape[0]):
        turned = jnp.transpose(oper_sum[relation, :, MAIN:])
        oper_out[relation, :D, :] = oper_sum[relation, :D, :MAIN]
        oper_out[relation, D:, :] = jnp.zeros((WIDE - D, MAIN), F32)
        oper_out[relation, D : D + REST, :] = turned[:REST, :MAIN]
        oper_out[relation, D + REST : D + 2 * REST, :128] = turned[:REST, MAIN:]


def bucket(packed, left_part, right_part, operators):
    groups = lax.axis_size("shard")
    total, _ = packed.shape
    packs = left_part.shape[0]
    part = packs - groups * REST
    whole = lambda shape: pl.BlockSpec(shape, lambda i: (0,) * len(shape))
    nrel = operators.shape[0]
    return pl.pallas_call(
        functools.partial(bucket_kernel, groups, total // groups),
        grid=(1,),
        in_specs=[
            pl.BlockSpec((total, 128), lambda i: (0, 3), memory_space=pltpu.SMEM),
            whole(packed.shape),
            whole(left_part.shape),
            whole(right_part.shape),
            whole(operators.shape),
        ],
        out_specs=[whole((packs, MAIN)), whole((packs, MAIN)), whole((nrel, WIDE, MAIN))],
        out_shape=[
            jax.ShapeDtypeStruct((packs, MAIN), BF),
            jax.ShapeDtypeStruct((packs, MAIN), BF),
            jax.ShapeDtypeStruct((nrel, WIDE, MAIN), F32),
        ],
        scratch_shapes=[
            pltpu.VMEM((part, WIDE), BF),
            pltpu.VMEM((part, WIDE), BF),
            pltpu.VMEM((nrel, WIDE, WIDE), BF),
            pltpu.VMEM((part, WIDE), F32),
            pltpu.VMEM((part, WIDE), F32),
            pltpu.VMEM((nrel, WIDE, WIDE), F32),
            pltpu.VMEM((128, WIDE), F32),
        ],
        compiler_params=pltpu.CompilerParams(vmem_limit_bytes=48 * 1024 * 1024),
        name="bucket",
    )(packed, packed, left_part, right_part, operators)


def update_kernel(
    lhs, lhs_acc, lhs_grad, rhs, rhs_acc, rhs_grad, operators, operator_acc, oper_grad,
    new_lhs, new_lhs_acc, new_rhs, new_rhs_acc, new_operators, new_operator_acc, turn, states,
):
    def squares(block):
        return jnp.sum(block * block, axis=1, keepdims=True)

    def step(main, rest, state_row):
        mean = (squares(main) + squares(rest)) * (1.0 / D)
        state = as_column(state_row) + mean
        root = jnp.sqrt(state)
        wide = jnp.concatenate([root] * (MAIN // 128), axis=1)
        return state, LEARN_RATE * main / wide, LEARN_RATE * rest / root

    tables = (
        (lhs, lhs_acc, lhs_grad, new_lhs, new_lhs_acc),
        (rhs, rhs_acc, rhs_grad, new_rhs, new_rhs_acc),
    )
    turn[...] = jnp.zeros_like(turn)
    for table, state_in, grad, new, new_state in tables:
        rows = table.shape[0]
        turn[:REST, :rows] = grad[rows:, :rows].astype(F32)
        rest = jnp.transpose(turn[:, :rows])
        state, main_step, rest_step = step(grad[:rows, :].astype(F32), rest, state_in[...])
        new[:, :MAIN] = (table[:, :MAIN].astype(F32) - main_step).astype(BF)
        new[:, MAIN:] = (table[:, MAIN:].astype(F32) - rest_step[:, :REST]).astype(BF)
        new_state[...] = jnp.transpose(state)[:1, :]
    states[...] = jnp.ones_like(states)
    states[: operators.shape[0], :D] = operator_acc[...]
    for r in range(operators.shape[0]):
        turn[:REST, :MAIN] = oper_grad[r, D : D + REST, :].astype(F32)
        turn[:REST, MAIN:] = oper_grad[r, D + REST : D + 2 * REST, :128].astype(F32)
        rest = jnp.transpose(turn[...])
        main = oper_grad[r].astype(F32)
        state, main_step, rest_step = step(main, rest, states[r : r + 1, :])
        new_operators[r, :, :MAIN] = operators[r, :, :MAIN] - main_step[:D]
        new_operators[r, :, MAIN:] = operators[r, :, MAIN:] - rest_step[:D, :REST]
        new_operator_acc[r : r + 1, :] = jnp.transpose(state)[:1, :D]


def update(*arrays):
    lhs, lhs_acc, _, rhs, rhs_acc, _, operators, operator_acc, _ = arrays
    vmem = pl.BlockSpec(memory_space=pltpu.VMEM)
    outs = (lhs, lhs_acc, rhs, rhs_acc, operators, operator_acc)
    return pl.pallas_call(
        update_kernel,
        in_specs=[vmem] * 9,
        out_specs=[vmem] * 6,
        out_shape=[jax.ShapeDtypeStruct(x.shape, x.dtype) for x in outs],
        scratch_shapes=[pltpu.VMEM((128, WIDE), F32), pltpu.VMEM((8, WIDE), F32)],
        compiler_params=pltpu.CompilerParams(vmem_limit_bytes=32 * 1024 * 1024),
        name="update",
    )(*arrays)


def per_device(
    lhs_emb,
    lhs_acc,
    rhs_emb,
    rhs_acc,
    operators,
    operator_acc,
    partner_mask,
    edge_lhs,
    edge_rhs,
    negatives,
    block_relation,
    edge_count,
):
    blocks = block_relation.shape[0]
    lane = lax.broadcasted_iota(jnp.int32, (blocks, 128), 1)
    info = jnp.where(lane == 0, block_relation[:, None], edge_count[0])
    packed = jnp.concatenate([edge_lhs, edge_rhs, negatives, info], axis=1)
    lists, left_part, right_part = collect(partner_mask, packed, lhs_emb, rhs_emb)
    grad_left, grad_right, grad_oper = bucket(lists, left_part, right_part, operators)
    own_right, own_left, total_oper = reduce(partner_mask, grad_right, grad_left, grad_oper)
    as_row = lambda state: state.reshape(1, -1)
    new_lhs, new_lhs_acc, new_rhs, new_rhs_acc, new_operators, new_operator_acc = update(
        lhs_emb, as_row(lhs_acc), own_left, rhs_emb, as_row(rhs_acc), own_right,
        operators, operator_acc, total_oper,
    )
    return (
        new_lhs,
        new_lhs_acc.reshape(-1),
        new_rhs,
        new_rhs_acc.reshape(-1),
        new_operators,
        new_operator_acc,
    )


def solution(mesh):
    rows = P(("dom", "shard"), None)
    flat = P(("dom", "shard"))
    in_specs = (rows, flat, rows, flat, P(), P(), P(), rows, rows, rows, flat, flat)
    out_specs = (rows, flat, rows, flat, P(), P())
    return jax.shard_map(
        per_device, mesh=mesh, in_specs=in_specs, out_specs=out_specs, check_vma=False
    )
```

```python
import functools

import jax
import jax.numpy as jnp
from jax import lax
from jax.experimental import pallas as pl
from jax.experimental.pallas import tpu as pltpu
from jax.sharding import PartitionSpec as P

D = 400
WIDE = 512
MAIN = 384
REST = D - MAIN
SPAN = 128
LEARN_RATE = 0.1
BF = jnp.bfloat16
F32 = jnp.float32
MESH = pl.DeviceIdType.MESH


def flip(position, bit):
    return position + bit - 2 * bit * ((position // bit) % 2)


def partners(groups):
    dom, shard = lax.axis_index("dom"), lax.axis_index("shard")
    levels = [{"dom": flip(dom, 1 << l)} for l in range(groups.bit_length() - 1)]
    return levels, {"shard": flip(shard, 1)}, {"shard": flip(shard, 2)}


def is_home():
    return lax.axis_index("dom") % 2 == lax.axis_index("shard") // 2


def meet(others):
    barrier = pltpu.get_barrier_semaphore()
    for other in others:
        pl.semaphore_signal(barrier, inc=1, device_id=other, device_id_type=MESH)
    pl.semaphore_wait(barrier, len(others))


def level_orders(levels):
    order = list(range(levels))
    return [order, order[:1] + order[1:][::-1]]


def remote(src, dst, send_sem, recv_sem, other):
    return pltpu.make_async_remote_copy(
        src_ref=src,
        dst_ref=dst,
        send_sem=send_sem,
        recv_sem=recv_sem,
        device_id=other,
        device_id_type=MESH,
    )


def halves(size):
    first = (size // 2 + 15) // 16 * 16
    return ((0, first), (first, size - first))


class Swaps:
    def __init__(self, levels, mask, held, came, send_sem, recv_sem, size):
        self.levels, self.mask, self.held, self.came = levels, mask, held, came
        self.send_sem, self.recv_sem = send_sem, recv_sem
        self.orders = level_orders(len(levels))
        self.parts = halves(size)

    def slot(self, ref, half, step):
        return ref.at[half, step, pl.ds(0, self.parts[half][1])]

    def copy(self, half, step):
        return remote(
            self.slot(self.held, half, step),
            self.slot(self.came, half, step),
            self.send_sem.at[half, step],
            self.recv_sem.at[half, step],
            self.levels[self.orders[half][step]],
        )

    def start(self, step):
        for half in range(2):
            self.copy(half, step).start()

    def end(self, step):
        for half in range(2):
            self.copy(half, step).wait()
            bit = 1 << self.orders[half][step]
            flag = (self.mask[0] // bit) % 2
            came = self.slot(self.came, half, step)[...].astype(F32)
            wide = jnp.full(came.shape, flag, jnp.int32)
            held = self.slot(self.held, half, step)[...].astype(F32)
            self.slot(self.held, half, step + 1)[...] = jnp.where(wide == 1, came, held).astype(BF)
            if step + 1 < len(self.levels):
                self.copy(half, step + 1).start()

    def put(self, rows):
        for half, (at, size) in enumerate(self.parts):
            self.slot(self.held, half, 0)[...] = rows[at : at + size, :].astype(BF)

    def get(self, rows):
        for half, (at, size) in enumerate(self.parts):
            rows[at : at + size, :] = self.slot(self.held, half, len(self.levels))[...]


def shard_part(ref, j):
    at = lax.axis_index("shard")
    for bit in (1, 2):
        if j & bit:
            at = flip(at, bit)
    return ref.at[at]


def collect_kernel(
    groups, mask, relation, count, edge_lhs, edge_rhs, negatives, left, right, all_lists, all_left, all_right,
    held, came, fetched, lists, dsend, drecv, zsend, csend, recv,
):
    levels, near, far = partners(groups)
    core = levels[0]
    home = is_home()
    away = jnp.logical_not(home)
    sources = (lists, left, fetched)
    totals = (all_lists, all_left, all_right)

    def piece(t, j):
        return shard_part(totals[t], j)

    def to_near(t, j):
        return remote(piece(t, j), piece(t, j), zsend.at[t, j], recv.at[t, j + 1], near)

    def to_core(t, j):
        return remote(piece(t, j), piece(t, j), csend.at[t, j], recv.at[t, j], core)

    def to_far(t):
        return remote(sources[t], piece(t, 0), zsend.at[t, 0], recv.at[t, 2], far)

    def begin(t):
        @pl.when(home)
        def _():
            piece(t, 0)[...] = sources[t][...]
            to_near(t, 0).start()
            to_core(t, 0).start()

        @pl.when(away)
        def _():
            to_far(t).start()

    def relay(t):
        @pl.when(home)
        def _():
            to_core(t, 2).wait_recv()
            to_near(t, 2).start()
            to_core(t, 2).start()

    def spread(t):
        @pl.when(home)
        def _():
            for j in (1, 3):
                to_core(t, j).wait_recv()
                to_core(t, j).start()

    def finish(t):
        @pl.when(home)
        def _():
            for j in (0, 2):
                to_near(t, j).wait_send()
            for j in range(4):
                to_core(t, j).wait_send()

        @pl.when(away)
        def _():
            to_far(t).wait_send()
            for j in range(4):
                to_core(t, j).wait_recv()

    swaps = Swaps(levels, mask, held, came, dsend, drecv, right.shape[0])
    swaps.put(right)
    blocks = lists.shape[0]
    for at, part in enumerate((edge_lhs, edge_rhs, negatives)):
        lists[:, at * 128 : (at + 1) * 128] = part[...]
    rows = lax.broadcasted_iota(jnp.int32, (blocks, 128), 0)
    lanes = lax.broadcasted_iota(jnp.int32, (blocks, 128), 1)
    info = jnp.full((blocks, 128), count[0], jnp.int32)
    for block in range(blocks):
        info = jnp.where((rows == block) & (lanes == 0), relation[block], info)
    lists[:, 384:] = info
    meet(levels + [near, far])
    swaps.start(0)
    begin(0)
    begin(1)
    for step in range(len(levels)):
        swaps.end(step)
        if step == 0:
            relay(0)
        if step == min(1, len(levels) - 1):
            relay(1)
    swaps.get(fetched)
    begin(2)
    spread(0)
    spread(1)
    relay(2)
    spread(2)
    for t in range(3):
        finish(t)


def collect(mask, relation, count, edge_lhs, edge_rhs, negatives, left, right):
    groups, shards = lax.axis_size("dom"), lax.axis_size("shard")
    width, rows = left.shape
    steps = groups.bit_length() - 1
    blocks = edge_lhs.shape[0]
    half = halves(width)[0][1]
    vmem = pl.BlockSpec(memory_space=pltpu.VMEM)
    smem = pl.BlockSpec(memory_space=pltpu.SMEM)
    dma = pltpu.SemaphoreType.DMA
    return pl.pallas_call(
        functools.partial(collect_kernel, groups),
        in_specs=[smem] * 3 + [vmem] * 5,
        out_specs=[vmem] * 3,
        out_shape=[
            jax.ShapeDtypeStruct((shards, blocks, 512), jnp.int32),
            jax.ShapeDtypeStruct((shards, width, rows), BF),
            jax.ShapeDtypeStruct((shards, width, rows), BF),
        ],
        scratch_shapes=[
            pltpu.VMEM((2, steps + 1, half, rows), BF),
            pltpu.VMEM((2, steps, half, rows), BF),
            pltpu.VMEM((width, rows), BF),
            pltpu.VMEM((blocks, 512), jnp.int32),
            dma((2, steps)),
            dma((2, steps)),
            dma((3, 4)),
            dma((3, 4)),
            dma((3, 4)),
        ],
        compiler_params=pltpu.CompilerParams(
            collective_id=0, has_side_effects=True, vmem_limit_bytes=32 * 1024 * 1024
        ),
        name="collect",
    )(mask, relation, count, edge_lhs, edge_rhs, negatives, left, right)


def reduce_kernel(
    groups, mask, right, left, oper, own_right, own_left, oper_total,
    held, came, core_in, near_in, far_in, out_going, own_sum, piece_in, leaving, work,
    dsend, drecv, csend, crecv, nsend, nrecv, fsend, frecv, osend, orecv, gsend, grecv,
):
    levels, near, far = partners(groups)
    core = levels[0]
    home = is_home()
    away = jnp.logical_not(home)
    totals = (right, left)
    dom, shard = lax.axis_index("dom"), lax.axis_index("shard")

    def to_core(t, j):
        return remote(
            shard_part(totals[t], j), core_in.at[t, j], csend.at[t, j], crecv.at[t, j], core
        )

    def to_near(t, j):
        return remote(
            out_going.at[t, j], near_in.at[t, j // 2], nsend.at[t, j // 2], nrecv.at[t, j // 2], near
        )

    def to_far(t):
        return remote(out_going.at[t, 2], far_in.at[t], fsend.at[t], frecv.at[t], far)

    def begin(t):
        @pl.when(away)
        def _():
            for j in (1, 3, 0, 2):
                to_core(t, j).start()

    def pair_sum(t, j):
        return shard_part(totals[t], j)[...].astype(F32) + core_in[t, j].astype(F32)

    def first(t):
        @pl.when(home)
        def _():
            for j in (1, 3):
                to_core(t, j).wait_recv()
                out_going[t, j] = pair_sum(t, j).astype(BF)
                to_near(t, j).start()

    def second(t):
        @pl.when(home)
        def _():
            for j in (2, 0):
                to_core(t, j).wait_recv()
                to_near(t, j).wait_recv()
                total = pair_sum(t, j) + near_in[t, j // 2].astype(F32)
                if j == 2:
                    out_going[t, 2] = total.astype(BF)
                    to_far(t).start()
                else:
                    own_sum[t] = total

    def third(t):
        @pl.when(away)
        def _():
            to_far(t).wait_recv()
            own_sum[t] = far_in[t].astype(F32)

    def finish(t):
        @pl.when(home)
        def _():
            for j in (1, 3):
                to_near(t, j).wait_send()
            to_far(t).wait_send()

        @pl.when(away)
        def _():
            for j in range(4):
                to_core(t, j).wait_send()

    every = levels + [near, far]
    bits = [(dom // (1 << l)) % 2 for l in range(len(levels))] + [shard % 2, (shard // 2) % 2]
    last = len(every)
    tail = list(range(len(levels), last))
    chains = [order + tail for order in level_orders(len(levels))]
    nrel = work.shape[0]
    spans, lands = [work.shape[1]], [0]
    for step in range(last):
        spans.append(spans[-1] // 2 if spans[-1] >= 32 else spans[-1])
        lands.append(lands[-1] + spans[-1])
    starts = []
    for r in range(nrel):
        at = [shard * 0]
        for step in range(last):
            halves = spans[step + 1] < spans[step]
            at.append(at[-1] + bits[chains[r % 2][step]] * spans[step + 1] if halves else at[-1])
        starts.append(at)

    def window(ref, r, start, span):
        return ref.at[r, pl.ds(pl.multiple_of(start, 16), span)]

    def oper_copy(r, step):
        land = pl.ds(lands[step], spans[step + 1])
        return remote(
            leaving.at[r, land],
            piece_in.at[r, land],
            osend.at[r, step],
            orecv.at[r, step],
            every[chains[r % 2][step]],
        )

    def oper_start(step):
        for r in range(nrel):
            span, start = spans[step + 1], starts[r][step]
            if span < spans[step]:
                start = start + (1 - bits[chains[r % 2][step]]) * span
            leaving[r, pl.ds(lands[step], span)] = window(work, r, start, span)[...].astype(BF)
            oper_copy(r, step).start()

    def oper_end(step):
        for r in range(nrel):
            oper_copy(r, step).wait()
            span = spans[step + 1]
            land = pl.ds(lands[step], span)
            own = window(work, r, starts[r][step + 1], span)
            kept = own[...] if span < spans[step] else leaving[r, land].astype(F32)
            own[...] = kept + piece_in[r, land].astype(F32)

    def back_copy(r, step):
        part = window(oper_total, r, starts[r][step + 1], spans[step + 1])
        return remote(part, part, gsend.at[r, step], grecv.at[r, step], every[chains[r % 2][step]])

    swaps = Swaps(levels, mask, held, came, dsend, drecv, own_right.shape[0])
    work[...] = oper[...]
    meet(every)
    begin(0)
    oper_start(0)
    begin(1)
    todo = {
        0: lambda: (first(0), first(1)),
        1: lambda: second(0),
        2: lambda: (third(0), swaps.put(own_sum.at[0]), swaps.start(0), second(1)),
    }
    for step in range(last):
        if step in todo:
            todo[step]()
        if 3 <= step < 3 + len(levels):
            swaps.end(step - 3)
        oper_end(step)
        if step + 1 < last:
            oper_start(step + 1)
    for r in range(nrel):
        final = window(work, r, starts[r][-1], spans[-1])[...]
        window(oper_total, r, starts[r][-1], spans[-1])[...] = final.astype(BF)
    swap = last - 3
    for step in reversed(range(last)):
        if spans[step + 1] == spans[step]:
            continue
        for r in range(nrel):
            back_copy(r, step).start()
        if swap < len(levels):
            swaps.end(swap)
            swap += 1
        for r in range(nrel):
            back_copy(r, step).wait()
    for rest in range(swap, len(levels)):
        swaps.end(rest)
    swaps.get(own_right)
    third(1)
    own_left[...] = own_sum[1]
    for t in range(2):
        finish(t)


def reduce(mask, grad_right, grad_left, grad_oper):
    groups, shards = lax.axis_size("dom"), lax.axis_size("shard")
    _, width, rows = grad_left.shape
    half = halves(width)[0][1]
    steps = groups.bit_length() - 1
    every = steps + 2
    nrel = grad_oper.shape[0]
    vmem = pl.BlockSpec(memory_space=pltpu.VMEM)
    dma = pltpu.SemaphoreType.DMA
    return pl.pallas_call(
        functools.partial(reduce_kernel, groups),
        in_specs=[pl.BlockSpec(memory_space=pltpu.SMEM)] + [vmem] * 3,
        out_specs=[vmem] * 3,
        out_shape=[
            jax.ShapeDtypeStruct((width, rows), BF),
            jax.ShapeDtypeStruct((width, rows), F32),
            jax.ShapeDtypeStruct(grad_oper.shape, BF),
        ],
        scratch_shapes=[
            pltpu.VMEM((2, steps + 1, half, rows), BF),
            pltpu.VMEM((2, steps, half, rows), BF),
            pltpu.VMEM((2, 4, width, rows), BF),
            pltpu.VMEM((2, 2, width, rows), BF),
            pltpu.VMEM((2, width, rows), BF),
            pltpu.VMEM((2, 4, width, rows), BF),
            pltpu.VMEM((2, width, rows), F32),
            pltpu.VMEM((nrel, grad_oper.shape[1] + 16 * every, MAIN), BF),
            pltpu.VMEM((nrel, grad_oper.shape[1] + 16 * every, MAIN), BF),
            pltpu.VMEM(grad_oper.shape, F32),
            dma((2, steps)),
            dma((2, steps)),
            dma((2, 4)),
            dma((2, 4)),
            dma((2, 2)),
            dma((2, 2)),
            dma((2,)),
            dma((2,)),
            dma((nrel, every)),
            dma((nrel, every)),
            dma((nrel, every)),
            dma((nrel, every)),
        ],
        compiler_params=pltpu.CompilerParams(
            collective_id=1, has_side_effects=True, vmem_limit_bytes=40 * 1024 * 1024
        ),
        name="reduce",
    )(mask, grad_right, grad_left, grad_oper)


def dot(a, b, dims):
    return lax.dot_general(a, b, (dims, ((), ())), preferred_element_type=F32)


def as_column(index_row):
    return jnp.transpose(jnp.broadcast_to(index_row, (128, index_row.shape[1])))


def gather_rows(index_row, table):
    part = table.shape[0]
    column = as_column(index_row)
    lanes = lax.broadcasted_iota(jnp.int32, column.shape, 1)
    shifted = column - lanes
    hot = jnp.concatenate(
        [jnp.where(shifted == c * 128, 1.0, 0.0).astype(BF) for c in range(part // 128)], axis=1
    )
    return dot(hot, table[...], ((1,), (0,))).astype(BF)


def scatter_rows(index_row, grads, total):
    part = total.shape[0]
    step = 256
    rows = lax.broadcasted_iota(jnp.int32, (step, index_row.shape[1]), 0)
    shifted = jnp.broadcast_to(index_row, rows.shape) - rows
    for c in range(part // step):
        hot = jnp.where(shifted == c * step, 1.0, 0.0).astype(BF)
        total[pl.ds(c * step, step), :] += dot(hot, grads, ((1,), (0,)))


def bucket_kernel(
    groups,
    info,
    index,
    left_in,
    right_in,
    oper_in,
    left_out,
    right_out,
    oper_out,
    left,
    right,
    oper,
    left_sum,
    right_sum,
    oper_sum,
    turn,
):
    me = (lax.axis_index("shard") % 2) * 2 + lax.axis_index("dom") % 2
    rows = left.shape[0] // groups
    for wide, packed in ((left, left_in), (right, right_in)):
        turn[...] = jnp.zeros_like(turn)
        for g in range(groups):
            turn[:D, :] = packed[g].astype(F32)
            wide[g * rows : (g + 1) * rows, :] = jnp.transpose(turn[...]).astype(BF)
    oper[...] = jnp.zeros_like(oper)
    oper[:, :D, :D] = oper_in[...].astype(BF)
    left_sum[...] = jnp.zeros_like(left_sum)
    right_sum[...] = jnp.zeros_like(right_sum)
    oper_sum[...] = jnp.zeros_like(oper_sum)

    counts = [info[g, 0, 1] for g in range(groups)]
    starts = [jnp.int32(0)]
    for g in range(groups):
        starts.append(starts[-1] + (counts[g] + SPAN - 1) // SPAN)
    in_all = starts[-1]
    mine = (in_all - me + groups - 1) // groups

    def locate(step):
        slot = step * groups + me
        exists = slot < in_all
        slot = jnp.minimum(slot, in_all - 1)
        owner = jnp.int32(0)
        start = jnp.int32(0)
        count = counts[0]
        for g in range(1, groups):
            later = slot >= starts[g]
            owner = jnp.where(later, g, owner)
            start = jnp.where(later, starts[g], start)
            count = jnp.where(later, counts[g], count)
        within = slot - start
        live = jnp.where(exists, count - within * SPAN, 0)
        return owner, within, info[owner, within, 0], live

    def visit(pair, carry):
        left_ids, right_ids, left_grads, right_grads = [], [], [], []
        for half in range(2):
            owner, within, relation, live = locate(pair * 2 + half)
            row = index[owner, pl.ds(within, 1), :]
            left_id = row[:, :SPAN]
            right_id = row[:, SPAN : 3 * SPAN]
            low = oper[relation]
            left_rows = gather_rows(left_id, left)
            candidates = gather_rows(right_id, right)
            projected = dot(left_rows, low, ((1,), (0,))).astype(BF)
            scores = dot(projected, candidates, ((1,), (1,)))
            rows = lax.broadcasted_iota(jnp.int32, scores.shape, 0)
            columns = lax.broadcasted_iota(jnp.int32, scores.shape, 1)
            column_live = (columns < live) | (columns >= SPAN)
            masked = jnp.where(column_live, scores, -jnp.inf)
            row_top = jnp.max(masked, axis=1, keepdims=True)
            exp_scores = jnp.exp(masked - row_top)
            soft = exp_scores / jnp.sum(exp_scores, axis=1, keepdims=True)
            grad = soft - jnp.where(rows == columns, 1.0, 0.0)
            score_grad = jnp.where(rows < live, grad, 0.0).astype(BF)
            proj_grad = dot(score_grad, candidates, ((1,), (0,))).astype(BF)
            cand_grad = dot(score_grad, projected, ((0,), (0,)))
            left_grad = dot(proj_grad, low, ((1,), (1,)))
            oper_sum[relation] += dot(left_rows, proj_grad, ((0,), (0,)))
            left_ids.append(left_id)
            right_ids.append(right_id)
            left_grads.append(left_grad.astype(BF))
            right_grads.append(cand_grad.astype(BF))
        join = lambda parts, axis: jnp.concatenate(parts, axis=axis)
        scatter_rows(join(left_ids, 1), join(left_grads, 0), left_sum)
        scatter_rows(join(right_ids, 1), join(right_grads, 0), right_sum)
        return carry

    lax.fori_loop(0, (mine + 1) // 2, visit, 0)
    for total, out in ((left_sum, left_out), (right_sum, right_out)):
        for g in range(groups):
            out[g] = jnp.transpose(total[g * rows : (g + 1) * rows, :])[:D, :].astype(BF)
    for relation in range(oper_sum.shape[0]):
        turned = jnp.transpose(oper_sum[relation, :, MAIN:])
        oper_out[relation, :D, :] = oper_sum[relation, :D, :MAIN]
        oper_out[relation, D:, :] = jnp.zeros((WIDE - D, MAIN), F32)
        oper_out[relation, D : D + REST, :] = turned[:REST, :MAIN]
        oper_out[relation, D + REST : D + 2 * REST, :128] = turned[:REST, MAIN:]


def bucket(lists, left_part, right_part, operators):
    groups, blocks, _ = lists.shape
    _, width, rows = left_part.shape
    part = groups * rows
    whole = lambda shape: pl.BlockSpec(shape, lambda i: (0,) * len(shape))
    nrel = operators.shape[0]
    return pl.pallas_call(
        functools.partial(bucket_kernel, groups),
        grid=(1,),
        in_specs=[
            pl.BlockSpec((groups, blocks, 128), lambda i: (0, 0, 3), memory_space=pltpu.SMEM),
            whole(lists.shape),
            whole(left_part.shape),
            whole(right_part.shape),
            whole(operators.shape),
        ],
        out_specs=[whole(left_part.shape), whole(left_part.shape), whole((nrel, WIDE, MAIN))],
        out_shape=[
            jax.ShapeDtypeStruct(left_part.shape, BF),
            jax.ShapeDtypeStruct(left_part.shape, BF),
            jax.ShapeDtypeStruct((nrel, WIDE, MAIN), F32),
        ],
        scratch_shapes=[
            pltpu.VMEM((part, WIDE), BF),
            pltpu.VMEM((part, WIDE), BF),
            pltpu.VMEM((nrel, WIDE, WIDE), BF),
            pltpu.VMEM((part, WIDE), F32),
            pltpu.VMEM((part, WIDE), F32),
            pltpu.VMEM((nrel, WIDE, WIDE), F32),
            pltpu.VMEM((WIDE, rows), F32),
        ],
        compiler_params=pltpu.CompilerParams(vmem_limit_bytes=48 * 1024 * 1024),
        name="bucket",
    )(lists, lists, left_part, right_part, operators)


def update_kernel(
    lhs, lhs_acc, lhs_grad, rhs, rhs_acc, rhs_grad, operators, operator_acc, oper_grad,
    new_lhs, new_lhs_acc, new_rhs, new_rhs_acc, new_operators, new_operator_acc, turn, states,
):
    def squares(block):
        return jnp.sum(block * block, axis=1, keepdims=True)

    def step(main, rest, state_row):
        mean = (squares(main) + squares(rest)) * (1.0 / D)
        state = as_column(state_row) + mean
        root = jnp.sqrt(state)
        wide = jnp.concatenate([root] * (MAIN // 128), axis=1)
        return state, LEARN_RATE * main / wide, LEARN_RATE * rest / root

    tables = (
        (lhs, lhs_acc, lhs_grad, new_lhs, new_lhs_acc),
        (rhs, rhs_acc, rhs_grad, new_rhs, new_rhs_acc),
    )
    for table, state_in, grad, new, new_state in tables:
        rows = grad[...].astype(F32)
        state = state_in[...] + jnp.sum(rows * rows, axis=0, keepdims=True) * (1.0 / D)
        new[...] = (table[...].astype(F32) - LEARN_RATE * rows / jnp.sqrt(state)).astype(BF)
        new_state[...] = state
    turn[...] = jnp.zeros_like(turn)
    states[...] = jnp.ones_like(states)
    states[: operators.shape[0], :D] = operator_acc[...]
    for r in range(operators.shape[0]):
        turn[:REST, :MAIN] = oper_grad[r, D : D + REST, :].astype(F32)
        turn[:REST, MAIN:] = oper_grad[r, D + REST : D + 2 * REST, :128].astype(F32)
        rest = jnp.transpose(turn[...])
        main = oper_grad[r].astype(F32)
        state, main_step, rest_step = step(main, rest, states[r : r + 1, :])
        new_operators[r, :, :MAIN] = operators[r, :, :MAIN] - main_step[:D]
        new_operators[r, :, MAIN:] = operators[r, :, MAIN:] - rest_step[:D, :REST]
        new_operator_acc[r : r + 1, :] = jnp.transpose(state)[:1, :D]


def update(*arrays):
    lhs, lhs_acc, _, rhs, rhs_acc, _, operators, operator_acc, _ = arrays
    vmem = pl.BlockSpec(memory_space=pltpu.VMEM)
    outs = (lhs, lhs_acc, rhs, rhs_acc, operators, operator_acc)
    return pl.pallas_call(
        update_kernel,
        in_specs=[vmem] * 9,
        out_specs=[vmem] * 6,
        out_shape=[jax.ShapeDtypeStruct(x.shape, x.dtype) for x in outs],
        scratch_shapes=[pltpu.VMEM((128, WIDE), F32), pltpu.VMEM((8, WIDE), F32)],
        compiler_params=pltpu.CompilerParams(vmem_limit_bytes=32 * 1024 * 1024),
        name="update",
    )(*arrays)


def per_device(
    lhs_emb,
    lhs_acc,
    rhs_emb,
    rhs_acc,
    operators,
    operator_acc,
    partner_mask,
    edge_lhs,
    edge_rhs,
    negatives,
    block_relation,
    edge_count,
):
    lhs_turned, rhs_turned = lhs_emb.T, rhs_emb.T
    lists, left_part, right_part = collect(
        partner_mask, block_relation, edge_count, edge_lhs, edge_rhs, negatives, lhs_turned, rhs_turned
    )
    grad_left, grad_right, grad_oper = bucket(lists, left_part, right_part, operators)
    own_right, own_left, total_oper = reduce(partner_mask, grad_right, grad_left, grad_oper)
    as_row = lambda state: state.reshape(1, -1)
    new_lhs, new_lhs_acc, new_rhs, new_rhs_acc, new_operators, new_operator_acc = update(
        lhs_turned, as_row(lhs_acc), own_left, rhs_turned, as_row(rhs_acc), own_right,
        operators, operator_acc, total_oper,
    )
    return (
        new_lhs.T,
        new_lhs_acc.reshape(-1),
        new_rhs.T,
        new_rhs_acc.reshape(-1),
        new_operators,
        new_operator_acc,
    )


def solution(mesh):
    rows = P(("dom", "shard"), None)
    flat = P(("dom", "shard"))
    in_specs = (rows, flat, rows, flat, P(), P(), P(), rows, rows, rows, flat, flat)
    out_specs = (rows, flat, rows, flat, P(), P())
    return jax.shard_map(
        per_device, mesh=mesh, in_specs=in_specs, out_specs=out_specs, check_vma=False
    )
```

```python
import functools

import jax
import jax.numpy as jnp
from jax import lax
from jax.experimental import pallas as pl
from jax.experimental.pallas import tpu as pltpu
from jax.sharding import PartitionSpec as P

D = 400
WIDE = 512
MAIN = 384
REST = D - MAIN
SPAN = 128
LEARN_RATE = 0.1
BF = jnp.bfloat16
F32 = jnp.float32
MESH = pl.DeviceIdType.MESH


def flip(position, bit):
    return position + bit - 2 * bit * ((position // bit) % 2)


def partners(groups):
    dom, shard = lax.axis_index("dom"), lax.axis_index("shard")
    levels = [{"dom": flip(dom, 1 << l)} for l in range(groups.bit_length() - 1)]
    return levels, {"shard": flip(shard, 1)}, {"shard": flip(shard, 2)}


def is_home():
    return lax.axis_index("dom") % 2 == lax.axis_index("shard") // 2


def meet(others):
    barrier = pltpu.get_barrier_semaphore()
    for other in others:
        pl.semaphore_signal(barrier, inc=1, device_id=other, device_id_type=MESH)
    pl.semaphore_wait(barrier, len(others))


def level_orders(levels):
    order = list(range(levels))
    return [order, order[:1] + order[1:][::-1]]


def remote(src, dst, send_sem, recv_sem, other):
    return pltpu.make_async_remote_copy(
        src_ref=src,
        dst_ref=dst,
        send_sem=send_sem,
        recv_sem=recv_sem,
        device_id=other,
        device_id_type=MESH,
    )


def halves(size):
    first = (size // 2 + 15) // 16 * 16
    return ((0, first), (first, size - first))


class Swaps:
    def __init__(self, levels, mask, held, came, send_sem, recv_sem, size):
        self.levels, self.mask, self.held, self.came = levels, mask, held, came
        self.send_sem, self.recv_sem = send_sem, recv_sem
        self.orders = level_orders(len(levels))
        self.parts = halves(size)

    def slot(self, ref, half, step):
        return ref.at[half, step, pl.ds(0, self.parts[half][1])]

    def copy(self, half, step):
        return remote(
            self.slot(self.held, half, step),
            self.slot(self.came, half, step),
            self.send_sem.at[half, step],
            self.recv_sem.at[half, step],
            self.levels[self.orders[half][step]],
        )

    def start(self, step):
        for half in range(2):
            self.copy(half, step).start()

    def end(self, step):
        for half in range(2):
            self.copy(half, step).wait()
            bit = 1 << self.orders[half][step]
            flag = (self.mask[0] // bit) % 2
            came = self.slot(self.came, half, step)[...].astype(F32)
            wide = jnp.full(came.shape, flag, jnp.int32)
            held = self.slot(self.held, half, step)[...].astype(F32)
            self.slot(self.held, half, step + 1)[...] = jnp.where(wide == 1, came, held).astype(BF)
            if step + 1 < len(self.levels):
                self.copy(half, step + 1).start()

    def put(self, rows):
        for half, (at, size) in enumerate(self.parts):
            self.slot(self.held, half, 0)[...] = rows[at : at + size, :].astype(BF)

    def get(self, rows):
        for half, (at, size) in enumerate(self.parts):
            rows[at : at + size, :] = self.slot(self.held, half, len(self.levels))[...]


def shard_part(ref, j):
    at = lax.axis_index("shard")
    for bit in (1, 2):
        if j & bit:
            at = flip(at, bit)
    return ref.at[at]


def collect_kernel(
    groups, mask, relation, count, edge_lhs, edge_rhs, negatives, left_in, right_in, all_lists, all_left, all_right,
    held, came, fetched, lists, left, right, bring, dsend, drecv, zsend, csend, recv,
):
    levels, near, far = partners(groups)
    core = levels[0]
    home = is_home()
    away = jnp.logical_not(home)
    sources = (lists, left, fetched)
    totals = (all_lists, all_left, all_right)

    def piece(t, j):
        return shard_part(totals[t], j)

    def to_near(t, j):
        return remote(piece(t, j), piece(t, j), zsend.at[t, j], recv.at[t, j + 1], near)

    def to_core(t, j):
        return remote(piece(t, j), piece(t, j), csend.at[t, j], recv.at[t, j], core)

    def to_far(t):
        return remote(sources[t], piece(t, 0), zsend.at[t, 0], recv.at[t, 2], far)

    def begin(t):
        @pl.when(home)
        def _():
            piece(t, 0)[...] = sources[t][...]
            to_near(t, 0).start()
            to_core(t, 0).start()

        @pl.when(away)
        def _():
            to_far(t).start()

    def relay(t):
        @pl.when(home)
        def _():
            to_core(t, 2).wait_recv()
            to_near(t, 2).start()
            to_core(t, 2).start()

    def spread(t):
        @pl.when(home)
        def _():
            for j in (1, 3):
                to_core(t, j).wait_recv()
                to_core(t, j).start()

    def finish(t):
        @pl.when(home)
        def _():
            for j in (0, 2):
                to_near(t, j).wait_send()
            for j in range(4):
                to_core(t, j).wait_send()

        @pl.when(away)
        def _():
            to_far(t).wait_send()
            for j in range(4):
                to_core(t, j).wait_recv()

    swaps = Swaps(levels, mask, held, came, dsend, drecv, right.shape[0])
    brought = [pltpu.make_async_copy(right_in, right, bring.at[0])]
    brought.append(pltpu.make_async_copy(left_in, left, bring.at[1]))
    for at, part in enumerate((edge_lhs, edge_rhs, negatives)):
        brought.append(
            pltpu.make_async_copy(part, lists.at[:, pl.ds(at * 128, 128)], bring.at[2 + at])
        )
    for copy in brought:
        copy.start()
    blocks = lists.shape[0]
    rows = lax.broadcasted_iota(jnp.int32, (blocks, 128), 0)
    lanes = lax.broadcasted_iota(jnp.int32, (blocks, 128), 1)
    info = jnp.full((blocks, 128), count[0], jnp.int32)
    for block in range(blocks):
        info = jnp.where((rows == block) & (lanes == 0), relation[block], info)
    lists[:, 384:] = info
    meet(levels + [near, far])
    for copy in brought:
        copy.wait()
    swaps.put(right)
    swaps.start(0)
    begin(0)
    begin(1)
    for step in range(len(levels)):
        swaps.end(step)
        if step == 0:
            relay(0)
        if step == min(1, len(levels) - 1):
            relay(1)
    swaps.get(fetched)
    begin(2)
    spread(0)
    spread(1)
    relay(2)
    spread(2)
    for t in range(3):
        finish(t)


def collect(mask, relation, count, edge_lhs, edge_rhs, negatives, left, right):
    groups, shards = lax.axis_size("dom"), lax.axis_size("shard")
    width, rows = left.shape
    steps = groups.bit_length() - 1
    blocks = edge_lhs.shape[0]
    half = halves(width)[0][1]
    vmem = pl.BlockSpec(memory_space=pltpu.VMEM)
    smem = pl.BlockSpec(memory_space=pltpu.SMEM)
    dma = pltpu.SemaphoreType.DMA
    return pl.pallas_call(
        functools.partial(collect_kernel, groups),
        in_specs=[smem] * 3 + [pl.BlockSpec(memory_space=pltpu.HBM)] * 5,
        out_specs=[vmem] * 3,
        out_shape=[
            jax.ShapeDtypeStruct((shards, blocks, 512), jnp.int32),
            jax.ShapeDtypeStruct((shards, width, rows), BF),
            jax.ShapeDtypeStruct((shards, width, rows), BF),
        ],
        scratch_shapes=[
            pltpu.VMEM((2, steps + 1, half, rows), BF),
            pltpu.VMEM((2, steps, half, rows), BF),
            pltpu.VMEM((width, rows), BF),
            pltpu.VMEM((blocks, 512), jnp.int32),
            pltpu.VMEM((width, rows), BF),
            pltpu.VMEM((width, rows), BF),
            dma((5,)),
            dma((2, steps)),
            dma((2, steps)),
            dma((3, 4)),
            dma((3, 4)),
            dma((3, 4)),
        ],
        compiler_params=pltpu.CompilerParams(
            collective_id=0, has_side_effects=True, vmem_limit_bytes=32 * 1024 * 1024
        ),
        name="collect",
    )(mask, relation, count, edge_lhs, edge_rhs, negatives, left, right)


def reduce_kernel(
    groups, mask, right, left, oper, own_right, own_left, oper_total,
    held, came, core_in, near_in, far_in, out_going, own_sum, piece_in, leaving, work,
    dsend, drecv, csend, crecv, nsend, nrecv, fsend, frecv, osend, orecv, gsend, grecv,
):
    levels, near, far = partners(groups)
    core = levels[0]
    home = is_home()
    away = jnp.logical_not(home)
    totals = (right, left)
    dom, shard = lax.axis_index("dom"), lax.axis_index("shard")

    def to_core(t, j):
        return remote(
            shard_part(totals[t], j), core_in.at[t, j], csend.at[t, j], crecv.at[t, j], core
        )

    def to_near(t, j):
        return remote(
            out_going.at[t, j], near_in.at[t, j // 2], nsend.at[t, j // 2], nrecv.at[t, j // 2], near
        )

    def to_far(t):
        return remote(out_going.at[t, 2], far_in.at[t], fsend.at[t], frecv.at[t], far)

    def begin(t):
        @pl.when(away)
        def _():
            for j in (1, 3, 0, 2):
                to_core(t, j).start()

    def pair_sum(t, j):
        return shard_part(totals[t], j)[...].astype(F32) + core_in[t, j].astype(F32)

    def first(t):
        @pl.when(home)
        def _():
            for j in (1, 3):
                to_core(t, j).wait_recv()
                out_going[t, j] = pair_sum(t, j).astype(BF)
                to_near(t, j).start()

    def second(t):
        @pl.when(home)
        def _():
            for j in (2, 0):
                to_core(t, j).wait_recv()
                to_near(t, j).wait_recv()
                total = pair_sum(t, j) + near_in[t, j // 2].astype(F32)
                if j == 2:
                    out_going[t, 2] = total.astype(BF)
                    to_far(t).start()
                else:
                    own_sum[t] = total

    def third(t):
        @pl.when(away)
        def _():
            to_far(t).wait_recv()
            own_sum[t] = far_in[t].astype(F32)

    def finish(t):
        @pl.when(home)
        def _():
            for j in (1, 3):
                to_near(t, j).wait_send()
            to_far(t).wait_send()

        @pl.when(away)
        def _():
            for j in range(4):
                to_core(t, j).wait_send()

    stages = [[0]] + [list(range(l, min(l + 2, len(levels)))) for l in range(1, len(levels), 2)]
    places = []
    for bits in stages:
        places.append([(dom // (1 << l)) % 2 for l in bits])
    places.append([shard % 2, (shard // 2) % 2])

    def peer(stage, k):
        if stage == len(stages):
            return [near, far, {"shard": flip(flip(shard, 1), 2)}][k - 1]
        at = dom
        for n, l in enumerate(stages[stage]):
            if k >> n & 1:
                at = flip(at, 1 << l)
        return {"dom": at}

    def member(stage, k):
        return sum((1 - bit if k >> n & 1 else bit) << n for n, bit in enumerate(places[stage]))

    last = len(places)
    sizes = [1 << len(bits) for bits in places]
    nrel = work.shape[0]
    spans, lands, starts = [work.shape[1]], [0], [shard * 0]
    for stage in range(last):
        cut = spans[-1] // sizes[stage]
        spans.append(cut if cut >= 16 else spans[-1])
        halves_it = spans[-1] < spans[-2]
        starts.append(starts[-1] + member(stage, 0) * spans[-1] if halves_it else starts[-1])
        lands.append(lands[-1] + spans[-1] * (sizes[stage] - 1))

    def window(ref, r, start, span):
        return ref.at[r, pl.ds(pl.multiple_of(start, 16), span)]

    def land(stage, k):
        return pl.ds(lands[stage] + (k - 1) * spans[stage + 1], spans[stage + 1])

    def oper_copy(r, stage, k):
        return remote(
            leaving.at[r, land(stage, k)],
            piece_in.at[r, land(stage, k)],
            osend.at[r, stage, k],
            orecv.at[r, stage, k],
            peer(stage, k),
        )

    def oper_start(stage):
        span = spans[stage + 1]
        for k in range(sizes[stage] - 1, 0, -1):
            for r in range(nrel):
                start = starts[stage]
                if span < spans[stage]:
                    start = start + member(stage, k) * span
                leaving[r, land(stage, k)] = window(work, r, start, span)[...].astype(BF)
                oper_copy(r, stage, k).start()

    def oper_end(stage):
        span = spans[stage + 1]
        for r in range(nrel):
            for k in range(1, sizes[stage]):
                oper_copy(r, stage, k).wait()
            own = window(work, r, starts[stage + 1], span)
            came_in = [piece_in[r, land(stage, k)].astype(F32) for k in range(1, sizes[stage])]
            kept = own[...] if span < spans[stage] else leaving[r, land(stage, 1)].astype(F32)
            total = kept + came_in[0]
            if len(came_in) > 1:
                total = total + (came_in[1] + came_in[2])
            own[...] = total

    def back_copy(r, stage, k):
        part = window(oper_total, r, starts[stage + 1], spans[stage + 1])
        return remote(part, part, gsend.at[r, stage, k], grecv.at[r, stage, k], peer(stage, k))

    def back_recv(r, stage, k):
        part = window(oper_total, r, starts[stage] + member(stage, k) * spans[stage + 1], spans[stage + 1])
        return remote(part, part, gsend.at[r, stage, k], grecv.at[r, stage, k], peer(stage, k))

    swaps = Swaps(levels, mask, held, came, dsend, drecv, own_right.shape[0])
    work[...] = oper[...]
    meet([peer(stage, k) for stage in range(last) for k in range(1, sizes[stage])])
    rows_work = [
        lambda: first(0),
        lambda: (first(1), second(0)),
        lambda: (third(0), swaps.put(own_sum.at[0]), swaps.start(0), second(1)),
    ] + [functools.partial(swaps.end, level) for level in range(len(levels))]

    def rows_step():
        if rows_work:
            rows_work.pop(0)()

    begin(0)
    oper_start(0)
    begin(1)
    for stage in range(last):
        rows_step()
        oper_end(stage)
        if stage + 1 < last:
            oper_start(stage + 1)
    for r in range(nrel):
        final = window(work, r, starts[-1], spans[-1])[...]
        window(oper_total, r, starts[-1], spans[-1])[...] = final.astype(BF)
    for stage in reversed(range(last)):
        if spans[stage + 1] == spans[stage]:
            continue
        for k in range(sizes[stage] - 1, 0, -1):
            for r in range(nrel):
                back_copy(r, stage, k).start()
        rows_step()
        for k in range(1, sizes[stage]):
            for r in range(nrel):
                back_copy(r, stage, k).wait_send()
                back_recv(r, stage, k).wait_recv()
    while rows_work:
        rows_step()
    swaps.get(own_right)
    third(1)
    own_left[...] = own_sum[1]
    for t in range(2):
        finish(t)


def reduce(mask, grad_right, grad_left, grad_oper):
    groups, shards = lax.axis_size("dom"), lax.axis_size("shard")
    _, width, rows = grad_left.shape
    half = halves(width)[0][1]
    steps = groups.bit_length() - 1
    stages = 2 + steps // 2
    nrel = grad_oper.shape[0]
    vmem = pl.BlockSpec(memory_space=pltpu.VMEM)
    dma = pltpu.SemaphoreType.DMA
    return pl.pallas_call(
        functools.partial(reduce_kernel, groups),
        in_specs=[pl.BlockSpec(memory_space=pltpu.SMEM)] + [vmem] * 3,
        out_specs=[vmem] * 3,
        out_shape=[
            jax.ShapeDtypeStruct((width, rows), BF),
            jax.ShapeDtypeStruct((width, rows), F32),
            jax.ShapeDtypeStruct(grad_oper.shape, BF),
        ],
        scratch_shapes=[
            pltpu.VMEM((2, steps + 1, half, rows), BF),
            pltpu.VMEM((2, steps, half, rows), BF),
            pltpu.VMEM((2, 4, width, rows), BF),
            pltpu.VMEM((2, 2, width, rows), BF),
            pltpu.VMEM((2, width, rows), BF),
            pltpu.VMEM((2, 4, width, rows), BF),
            pltpu.VMEM((2, width, rows), F32),
            pltpu.VMEM((nrel, 2 * grad_oper.shape[1] + 64 * stages, MAIN), BF),
            pltpu.VMEM((nrel, 2 * grad_oper.shape[1] + 64 * stages, MAIN), BF),
            pltpu.VMEM(grad_oper.shape, F32),
            dma((2, steps)),
            dma((2, steps)),
            dma((2, 4)),
            dma((2, 4)),
            dma((2, 2)),
            dma((2, 2)),
            dma((2,)),
            dma((2,)),
            dma((nrel, stages, 4)),
            dma((nrel, stages, 4)),
            dma((nrel, stages, 4)),
            dma((nrel, stages, 4)),
        ],
        compiler_params=pltpu.CompilerParams(
            collective_id=1, has_side_effects=True, vmem_limit_bytes=40 * 1024 * 1024
        ),
        name="reduce",
    )(mask, grad_right, grad_left, grad_oper)


def dot(a, b, dims):
    return lax.dot_general(a, b, (dims, ((), ())), preferred_element_type=F32)


def as_column(index_row):
    return jnp.transpose(jnp.broadcast_to(index_row, (128, index_row.shape[1])))


def gather_rows(index_row, table):
    part = table.shape[0]
    column = as_column(index_row)
    lanes = lax.broadcasted_iota(jnp.int32, column.shape, 1)
    shifted = column - lanes
    hot = jnp.concatenate(
        [jnp.where(shifted == c * 128, 1.0, 0.0).astype(BF) for c in range(part // 128)], axis=1
    )
    return dot(hot, table[...], ((1,), (0,))).astype(BF)


def scatter_rows(index_row, grads, total):
    part = total.shape[0]
    step = 256
    rows = lax.broadcasted_iota(jnp.int32, (step, index_row.shape[1]), 0)
    shifted = jnp.broadcast_to(index_row, rows.shape) - rows
    for c in range(part // step):
        hot = jnp.where(shifted == c * step, 1.0, 0.0).astype(BF)
        total[pl.ds(c * step, step), :] += dot(hot, grads, ((1,), (0,)))


def bucket_kernel(
    groups,
    info,
    index,
    left_in,
    right_in,
    oper_in,
    left_out,
    right_out,
    oper_out,
    left,
    right,
    oper,
    left_sum,
    right_sum,
    oper_sum,
    turn,
    turned_oper,
):
    me = (lax.axis_index("shard") % 2) * 2 + lax.axis_index("dom") % 2
    rows = left.shape[0] // groups
    for wide, packed in ((left, left_in), (right, right_in)):
        turn[...] = jnp.zeros_like(turn)
        for g in range(groups):
            turn[:D, :] = packed[g].astype(F32)
            wide[g * rows : (g + 1) * rows, :] = jnp.transpose(turn[...]).astype(BF)
    oper[...] = jnp.zeros_like(oper)
    oper[:, :D, :D] = oper_in[...].astype(BF)
    for r in range(oper.shape[0]):
        turned_oper[r] = jnp.transpose(oper[r].astype(F32)).astype(BF)
    left_sum[...] = jnp.zeros_like(left_sum)
    right_sum[...] = jnp.zeros_like(right_sum)
    oper_sum[...] = jnp.zeros_like(oper_sum)

    counts = [info[g, 0, 1] for g in range(groups)]
    starts = [jnp.int32(0)]
    for g in range(groups):
        starts.append(starts[-1] + (counts[g] + SPAN - 1) // SPAN)
    in_all = starts[-1]
    mine = (in_all - me + groups - 1) // groups

    def locate(step):
        slot = step * groups + me
        exists = slot < in_all
        slot = jnp.minimum(slot, in_all - 1)
        owner = jnp.int32(0)
        start = jnp.int32(0)
        count = counts[0]
        for g in range(1, groups):
            later = slot >= starts[g]
            owner = jnp.where(later, g, owner)
            start = jnp.where(later, starts[g], start)
            count = jnp.where(later, counts[g], count)
        within = slot - start
        live = jnp.where(exists, count - within * SPAN, 0)
        return owner, within, info[owner, within, 0], live

    def visit(group, carry):
        each = range(2)
        where = [locate(group * 2 + n) for n in each]
        found = [index[owner, pl.ds(within, 1), :] for owner, within, _, _ in where]
        left_ids = [row[:, :SPAN] for row in found]
        right_ids = [row[:, SPAN : 3 * SPAN] for row in found]
        lows = [oper[relation] for _, _, relation, _ in where]
        join = lambda parts, axis: jnp.concatenate(parts, axis=axis)
        cut = lambda whole, size: [whole[n * size : (n + 1) * size] for n in each]
        left_rows = cut(gather_rows(join(left_ids, 1), left), SPAN)
        candidates = cut(gather_rows(join(right_ids, 1), right), 2 * SPAN)
        projected = [dot(left_rows[n], lows[n], ((1,), (0,))).astype(BF) for n in each]
        scores = [dot(projected[n], candidates[n], ((1,), (1,))) for n in each]
        rows = lax.broadcasted_iota(jnp.int32, scores[0].shape, 0)
        columns = lax.broadcasted_iota(jnp.int32, scores[0].shape, 1)
        lives = [live for _, _, _, live in where]
        masked = [
            jnp.where((columns < lives[n]) | (columns >= SPAN), scores[n], -jnp.inf) for n in each
        ]
        tops = [jnp.max(masked[n], axis=1, keepdims=True) for n in each]
        exp_scores = [jnp.exp(masked[n] - tops[n]) for n in each]
        sums = [jnp.sum(exp_scores[n], axis=1, keepdims=True) for n in each]
        target = jnp.where(rows == columns, 1.0, 0.0)
        score_grads = [
            jnp.where(rows < lives[n], exp_scores[n] / sums[n] - target, 0.0).astype(BF) for n in each
        ]
        proj_grads = [dot(score_grads[n], candidates[n], ((1,), (0,))).astype(BF) for n in each]
        right_grads = [dot(score_grads[n], projected[n], ((0,), (0,))).astype(BF) for n in each]
        left_grads = [dot(proj_grads[n], turned_oper[where[n][2]], ((1,), (0,))).astype(BF) for n in each]
        oper_grads = [dot(left_rows[n], proj_grads[n], ((0,), (0,))) for n in each]
        scatter_rows(join(left_ids, 1), join(left_grads, 0), left_sum)
        scatter_rows(join(right_ids, 1), join(right_grads, 0), right_sum)
        for n in each:
            oper_sum[where[n][2]] += oper_grads[n]
        return carry

    lax.fori_loop(0, (mine + 1) // 2, visit, 0)
    for total, out in ((left_sum, left_out), (right_sum, right_out)):
        for g in range(groups):
            out[g] = jnp.transpose(total[g * rows : (g + 1) * rows, :])[:D, :].astype(BF)
    for relation in range(oper_sum.shape[0]):
        turned = jnp.transpose(oper_sum[relation, :, MAIN:])
        oper_out[relation, :D, :] = oper_sum[relation, :D, :MAIN]
        oper_out[relation, D:, :] = jnp.zeros((WIDE - D, MAIN), F32)
        oper_out[relation, D : D + REST, :] = turned[:REST, :MAIN]
        oper_out[relation, D + REST : D + 2 * REST, :128] = turned[:REST, MAIN:]


def bucket(lists, left_part, right_part, operators):
    groups, blocks, _ = lists.shape
    _, width, rows = left_part.shape
    part = groups * rows
    whole = lambda shape: pl.BlockSpec(shape, lambda i: (0,) * len(shape))
    nrel = operators.shape[0]
    return pl.pallas_call(
        functools.partial(bucket_kernel, groups),
        grid=(1,),
        in_specs=[
            pl.BlockSpec((groups, blocks, 128), lambda i: (0, 0, 3), memory_space=pltpu.SMEM),
            whole(lists.shape),
            whole(left_part.shape),
            whole(right_part.shape),
            whole(operators.shape),
        ],
        out_specs=[whole(left_part.shape), whole(left_part.shape), whole((nrel, WIDE, MAIN))],
        out_shape=[
            jax.ShapeDtypeStruct(left_part.shape, BF),
            jax.ShapeDtypeStruct(left_part.shape, BF),
            jax.ShapeDtypeStruct((nrel, WIDE, MAIN), F32),
        ],
        scratch_shapes=[
            pltpu.VMEM((part, WIDE), BF),
            pltpu.VMEM((part, WIDE), BF),
            pltpu.VMEM((nrel, WIDE, WIDE), BF),
            pltpu.VMEM((part, WIDE), F32),
            pltpu.VMEM((part, WIDE), F32),
            pltpu.VMEM((nrel, WIDE, WIDE), F32),
            pltpu.VMEM((WIDE, rows), F32),
            pltpu.VMEM((nrel, WIDE, WIDE), BF),
        ],
        compiler_params=pltpu.CompilerParams(vmem_limit_bytes=48 * 1024 * 1024),
        name="bucket",
    )(lists, lists, left_part, right_part, operators)


def update_kernel(
    lhs, lhs_acc, lhs_grad, rhs, rhs_acc, rhs_grad, operators, operator_acc, oper_grad,
    new_lhs, new_lhs_acc, new_rhs, new_rhs_acc, new_operators, new_operator_acc, turn, states,
):
    def squares(block):
        return jnp.sum(block * block, axis=1, keepdims=True)

    def step(main, rest, state_row):
        mean = (squares(main) + squares(rest)) * (1.0 / D)
        state = as_column(state_row) + mean
        root = jnp.sqrt(state)
        wide = jnp.concatenate([root] * (MAIN // 128), axis=1)
        return state, LEARN_RATE * main / wide, LEARN_RATE * rest / root

    tables = (
        (lhs, lhs_acc, lhs_grad, new_lhs, new_lhs_acc),
        (rhs, rhs_acc, rhs_grad, new_rhs, new_rhs_acc),
    )
    for table, state_in, grad, new, new_state in tables:
        rows = grad[...].astype(F32)
        state = state_in[...] + jnp.sum(rows * rows, axis=0, keepdims=True) * (1.0 / D)
        new[...] = (table[...].astype(F32) - LEARN_RATE * rows / jnp.sqrt(state)).astype(BF)
        new_state[...] = state
    turn[...] = jnp.zeros_like(turn)
    states[...] = jnp.ones_like(states)
    states[: operators.shape[0], :D] = operator_acc[...]
    for r in range(operators.shape[0]):
        turn[:REST, :MAIN] = oper_grad[r, D : D + REST, :].astype(F32)
        turn[:REST, MAIN:] = oper_grad[r, D + REST : D + 2 * REST, :128].astype(F32)
        rest = jnp.transpose(turn[...])
        main = oper_grad[r].astype(F32)
        state, main_step, rest_step = step(main, rest, states[r : r + 1, :])
        new_operators[r, :, :MAIN] = operators[r, :, :MAIN] - main_step[:D]
        new_operators[r, :, MAIN:] = operators[r, :, MAIN:] - rest_step[:D, :REST]
        new_operator_acc[r : r + 1, :] = jnp.transpose(state)[:1, :D]


def update(*arrays):
    lhs, lhs_acc, _, rhs, rhs_acc, _, operators, operator_acc, _ = arrays
    vmem = pl.BlockSpec(memory_space=pltpu.VMEM)
    outs = (lhs, lhs_acc, rhs, rhs_acc, operators, operator_acc)
    return pl.pallas_call(
        update_kernel,
        in_specs=[vmem] * 9,
        out_specs=[vmem] * 6,
        out_shape=[jax.ShapeDtypeStruct(x.shape, x.dtype) for x in outs],
        scratch_shapes=[pltpu.VMEM((128, WIDE), F32), pltpu.VMEM((8, WIDE), F32)],
        compiler_params=pltpu.CompilerParams(vmem_limit_bytes=32 * 1024 * 1024),
        name="update",
    )(*arrays)


def per_device(
    lhs_emb,
    lhs_acc,
    rhs_emb,
    rhs_acc,
    operators,
    operator_acc,
    partner_mask,
    edge_lhs,
    edge_rhs,
    negatives,
    block_relation,
    edge_count,
):
    lhs_turned, rhs_turned = lhs_emb.T, rhs_emb.T
    lists, left_part, right_part = collect(
        partner_mask, block_relation, edge_count, edge_lhs, edge_rhs, negatives, lhs_turned, rhs_turned
    )
    grad_left, grad_right, grad_oper = bucket(lists, left_part, right_part, operators)
    own_right, own_left, total_oper = reduce(partner_mask, grad_right, grad_left, grad_oper)
    as_row = lambda state: state.reshape(1, -1)
    new_lhs, new_lhs_acc, new_rhs, new_rhs_acc, new_operators, new_operator_acc = update(
        lhs_turned, as_row(lhs_acc), own_left, rhs_turned, as_row(rhs_acc), own_right,
        operators, operator_acc, total_oper,
    )
    return (
        new_lhs.T,
        new_lhs_acc.reshape(-1),
        new_rhs.T,
        new_rhs_acc.reshape(-1),
        new_operators,
        new_operator_acc,
    )


def solution(mesh):
    rows = P(("dom", "shard"), None)
    flat = P(("dom", "shard"))
    in_specs = (rows, flat, rows, flat, P(), P(), P(), rows, rows, rows, flat, flat)
    out_specs = (rows, flat, rows, flat, P(), P())
    return jax.shard_map(
        per_device, mesh=mesh, in_specs=in_specs, out_specs=out_specs, check_vma=False
    )
```
